32 devices in a mesh: dp: 8 (over z, y), seq: 4 (over x, core).
Axes of the slice: x: 2, y: 2, z: 4, core: 2. Of those that a mesh axis runs over, the one named last changes fastest.
Arguments:
- block_input: bfloat16 [8, 4, 256, 1408], P('dp', 'seq'), may hold values from -6 to 6
- norm_gain: float32 [1408], replicated, may hold values from 0.5 to 1.5
- qkv_weight: bfloat16 [1408, 4224], replicated, may hold values from -0.15625 to 0.15625
- frame_clip: int32 [8, 4], P('dp', 'seq'), may hold values from 0 to 2, never falling along the last dimension, each value on 1 to 2 neighbouring positions
- out_grad: bfloat16 [8, 4, 256, 1408], P('dp', 'seq'), may hold values from -6 to 6
Outputs:
- input_grad: bfloat16 [8, 4, 256, 1408], P('dp', 'seq')
- weight_grad: float32 [1408, 1408], P(('dp', 'seq'))
- gain_grad: float32 [1408], replicated
The draws below stay inside these ranges and needn't reach their ends.
Inputs may be any that keep to these rules, and one draw needn't show every extreme that they name: `frame_clip`: in each group the frames hold clips 0 to 2 in order, each of 1 to 2 frames, one exactly 2.
All inputs are finite; a program needn't handle non-finite values.
Results may differ from the reference program's by a relative error of at most 0.018.
Values may be sent and summed in bfloat16 or wider, within the bound.
A program may use at most 128 MiB of HBM per device.

```python
import math
import jax
import jax.numpy as jnp
import numpy as np
from jax import lax

D = 1408
HEADS = 16
PATCHES = 256
GROUP_FRAMES = 4
GROUPS = 8
TOKENS = 8192
CLIPS = 3
MOST_FRAMES = 2


def steps_of(key, extent, shards, low, high):
    def one(position, blocks):
        steps = jax.random.uniform(jax.random.fold_in(jax.random.fold_in(key, 6), position), (blocks,), jnp.float32, low / len(shards), high / len(shards))
        return jnp.repeat(jnp.exp(steps), extent[position] // blocks).reshape((-1,) + (1,) * (len(extent) - position - 1))

    level = one(*shards[0])
    for cut in shards[1:]:
        level = level * one(*cut)
    return level


def length_profile(amount, total, bound, slope):
    portions = [(1 << 20) // math.isqrt(grade ** slope) + 1 for grade in range(2, amount + 1)]
    spare, counts = total - bound - (amount - 1), [1] * (amount - 1)
    while spare > 0:
        movable = [i for i in range(amount - 1) if counts[i] < bound]
        pool, remaining = sum([portions[i] for i in movable]), spare
        for i in movable:
            extra = min(bound - counts[i], max(1, remaining * portions[i] // pool), spare)
            counts[i] = counts[i] + extra
            spare = spare - extra
    return np.array([bound] + counts)


def uneven(own_key, number_of, total, limit, slope):
    if number_of == 2:
        one = jax.random.randint(own_key, (), max(1, total - limit), min(limit, total - 1) + 1)
        return jnp.stack([one, total - one])
    lengths = jnp.asarray(length_profile(number_of, total, limit, slope), jnp.int32)
    pairs = (number_of - 1) // 2
    donor, taker = lengths[1:1 + 2 * pairs:2], lengths[2:2 + 2 * pairs:2]
    room = jnp.minimum(donor - 1, limit - taker)
    shifted = jax.random.randint(jax.random.fold_in(own_key, 1), (pairs,), 0, 1 << 20) % (room + 1)
    lengths = lengths.at[1:1 + 2 * pairs:2].set(donor - shifted).at[2:2 + 2 * pairs:2].set(taker + shifted)
    return lengths[jax.random.permutation(jax.random.fold_in(own_key, 2), number_of)]


def scatter_about(own_key, dims, deviation, most, cuts=(), dtype=jnp.bfloat16):
    entries = deviation * jax.random.normal(own_key, dims, jnp.float32)
    if cuts:
        entries = entries * steps_of(own_key, dims, cuts, -0.22, 0.18)
    return jnp.clip(entries, -most, most).astype(dtype)


def setup_inputs(seed: int = 0) -> dict:
    arg_keys = jax.random.split(jax.random.key(seed), 6)
    return {
        "block_input": scatter_about(arg_keys[0], (GROUPS, GROUP_FRAMES, PATCHES, D), 1.0, 6.0, ((0, 8), (1, 4))),
        "norm_gain": jnp.clip(1.0 + 0.1 * jax.random.normal(arg_keys[1], (D,), jnp.float32), 0.5, 1.5),
        "qkv_weight": scatter_about(arg_keys[2], (D, 3 * D), D ** -0.5, 0.15625),
        "frame_clip": jax.vmap(lambda own: jnp.searchsorted(jnp.cumsum(uneven(own, CLIPS, GROUP_FRAMES, MOST_FRAMES, 1)), jnp.arange(GROUP_FRAMES), side="right"))(jax.random.split(arg_keys[3], GROUPS)).reshape((GROUPS, GROUP_FRAMES)).astype(jnp.int32),
        "out_grad": scatter_about(arg_keys[4], (GROUPS, GROUP_FRAMES, PATCHES, D), 1.0, 6.0, ((0, 8), (1, 4))),
    }


epsilon = 1e-06

def attention_grad(projected, incoming, same_clip):
    frames_all, positions, triple = projected.shape
    width = triple // 3
    head_dim = width // HEADS
    blocks = projected.astype(jnp.float32).reshape(frames_all, positions, 3, HEADS, head_dim)
    query_part = blocks[:, :, 0]
    key_part = blocks[:, :, 1]
    value_part = blocks[:, :, 2]
    outgrad = incoming.astype(jnp.float32).reshape(frames_all, positions, HEADS, head_dim)
    scaling = head_dim ** (-0.5)
    scores = jnp.einsum('fphd,gphd->phfg', query_part, key_part) * scaling
    largest = lax.optimization_barrier(jnp.max(jnp.where(same_clip, scores, -jnp.inf), axis=-1, keepdims=True))
    powers = jnp.where(same_clip, jnp.exp(scores - largest), 0.0)
    softmaxed = powers / lax.optimization_barrier(jnp.sum(powers, axis=-1, keepdims=True))
    rounded_probs = lax.optimization_barrier(softmaxed.astype(jnp.bfloat16)).astype(jnp.float32)
    d_value = jnp.einsum('phfg,fphd->gphd', rounded_probs, outgrad)
    d_probs = jnp.einsum('fphd,gphd->phfg', outgrad, value_part)
    row_dot = lax.optimization_barrier(jnp.sum(softmaxed * d_probs, axis=-1, keepdims=True))
    d_scores = (softmaxed * (d_probs - row_dot) * scaling).astype(jnp.bfloat16)
    d_scores = lax.optimization_barrier(d_scores).astype(jnp.float32)
    d_query = jnp.einsum('phfg,gphd->fphd', d_scores, key_part)
    d_key = jnp.einsum('phfg,fphd->gphd', d_scores, query_part)
    stacked = jnp.stack([d_query, d_key, d_value], axis=2)
    return stacked.reshape(frames_all, positions, triple).astype(jnp.bfloat16)

def reference(block_input, norm_gain, qkv_weight, frame_clip, out_grad):
    width = qkv_weight.shape[0]

    def group_backward(carry, inputs):
        weight_acc, gain_acc = carry
        frames_in, clip_ids, grads_in = inputs
        inputs_f = frames_in.astype(jnp.float32)
        centered = inputs_f - lax.optimization_barrier(jnp.mean(inputs_f, axis=-1, keepdims=True))
        inv_std = lax.rsqrt(lax.optimization_barrier(jnp.mean(centered * centered, axis=-1, keepdims=True)) + epsilon)
        normalized = centered * inv_std
        normed = (normalized * norm_gain).astype(jnp.bfloat16)
        normed_rows = normed.reshape(-1, width)
        projected = jnp.dot(normed_rows, qkv_weight, preferred_element_type=jnp.float32).astype(jnp.bfloat16)
        projected = projected.reshape(frames_in.shape[0], frames_in.shape[1], 3 * width)
        same_clip = clip_ids[:, None] == clip_ids[None, :]
        grads_qkv = attention_grad(projected, grads_in, same_clip)
        grad_rows = grads_qkv.reshape(-1, 3 * width)
        weight_acc = weight_acc + jnp.dot(normed_rows.T, grad_rows[:, 2 * width:], preferred_element_type=jnp.float32)
        d_normed = jnp.dot(grad_rows, qkv_weight.T, preferred_element_type=jnp.float32).reshape(frames_in.shape)
        gain_acc = gain_acc + lax.optimization_barrier(jnp.sum(d_normed * normalized, axis=(0, 1)))
        d_hat = d_normed * norm_gain
        first_mean = lax.optimization_barrier(jnp.mean(d_hat, axis=-1, keepdims=True))
        second_mean = lax.optimization_barrier(jnp.mean(d_hat * normalized, axis=-1, keepdims=True))
        input_grad = (inv_std * (d_hat - first_mean - normalized * second_mean)).astype(jnp.bfloat16)
        return ((weight_acc, gain_acc), input_grad)
    start_carry = (jnp.zeros((width, width), jnp.float32), jnp.zeros((width,), jnp.float32))
    (weight_sum, gain_sum), input_grad = lax.scan(group_backward, start_carry, (block_input, frame_clip, out_grad))
    factor = TOKENS ** (-0.5)
    return (input_grad, weight_sum * factor, gain_sum * factor)
```

```python
import jax
import jax.numpy as jnp
from jax import lax
from jax.experimental import pallas as pl
from jax.experimental.pallas import tpu as pltpu
from jax.sharding import PartitionSpec as P

HEADS = 16


epsilon = 1e-06


def attention_grad(projected, incoming, same_clip):
    frames_all, positions, triple = projected.shape
    width = triple // 3
    head_dim = width // HEADS
    blocks = projected.reshape(frames_all, positions, 3, HEADS, head_dim)
    query_part = blocks[:, :, 0]
    key_part = blocks[:, :, 1]
    value_part = blocks[:, :, 2]
    outgrad = incoming.reshape(frames_all, positions, HEADS, head_dim)
    scaling = head_dim ** (-0.5)
    scores = (
        jnp.einsum("fphd,gphd->phfg", query_part, key_part, preferred_element_type=jnp.float32)
        * scaling
    )
    largest = jnp.max(jnp.where(same_clip, scores, -jnp.inf), axis=-1, keepdims=True)
    powers = jnp.where(same_clip, jnp.exp(scores - largest), 0.0)
    softmaxed = powers / jnp.sum(powers, axis=-1, keepdims=True)
    rounded_probs = softmaxed.astype(jnp.bfloat16)
    d_value = jnp.einsum(
        "phfg,fphd->gphd", rounded_probs, outgrad, preferred_element_type=jnp.float32
    )
    d_probs = jnp.einsum("fphd,gphd->phfg", outgrad, value_part, preferred_element_type=jnp.float32)
    row_dot = jnp.sum(softmaxed * d_probs, axis=-1, keepdims=True)
    d_scores = (softmaxed * (d_probs - row_dot) * scaling).astype(jnp.bfloat16)
    d_query = jnp.einsum("phfg,gphd->fphd", d_scores, key_part, preferred_element_type=jnp.float32)
    d_key = jnp.einsum("phfg,fphd->gphd", d_scores, query_part, preferred_element_type=jnp.float32)
    stacked = jnp.stack([d_query, d_key, d_value], axis=2)
    return stacked.reshape(frames_all, positions, triple).astype(jnp.bfloat16)


def transpose_product(grad_rows, qkv_weight):
    return lax.dot_general(
        grad_rows, qkv_weight, (((1,), (1,)), ((), ())), preferred_element_type=jnp.float32
    )


def shards(block_input, norm_gain, qkv_weight, frame_clip, out_grad):
    frames_dev = block_input.shape[1]
    patches = block_input.shape[2]
    width = block_input.shape[3]
    seq_count = lax.axis_size("seq")
    group_count = lax.axis_size("dp")
    local_pos = patches // seq_count
    factor = (frames_dev * patches * seq_count * group_count) ** (-0.5)
    inputs_f = block_input[0].astype(jnp.float32)
    centered = inputs_f - jnp.mean(inputs_f, axis=-1, keepdims=True)
    inv_std = lax.rsqrt(jnp.mean(centered * centered, axis=-1, keepdims=True) + epsilon)
    normalized = centered * inv_std
    normed = (normalized * norm_gain).astype(jnp.bfloat16)
    clip_ids = lax.all_gather(frame_clip, "seq", axis=1, tiled=True)[0]
    same_clip = clip_ids[:, None] == clip_ids[None, :]
    grad_split = out_grad[0].reshape(frames_dev, seq_count, local_pos, width)
    projected = jnp.dot(normed.reshape(-1, width), qkv_weight, preferred_element_type=jnp.float32)
    projected = projected.astype(jnp.bfloat16).reshape(frames_dev, seq_count, local_pos, 3 * width)
    moved_proj = lax.all_to_all(projected, "seq", split_axis=1, concat_axis=0, tiled=True)
    incoming = lax.all_to_all(grad_split, "seq", split_axis=1, concat_axis=0, tiled=True)
    grads_frames = attention_grad(moved_proj[:, 0], incoming[:, 0], same_clip)[:, None]
    grads_qkv = lax.all_to_all(grads_frames, "seq", split_axis=0, concat_axis=1, tiled=True)
    rows_x = normed.reshape(-1, width)
    rows_g = grads_qkv.reshape(-1, 3 * width)
    d_normed = transpose_product(rows_g, qkv_weight).reshape(frames_dev, patches, width)
    value_rows = rows_g[:, 2 * width :]
    weight_sum = lax.psum_scatter(
        lax.dot_general(
            rows_x, value_rows, (((0,), (0,)), ((), ())), preferred_element_type=jnp.float32
        ),
        ("dp", "seq"),
        scatter_dimension=0,
        tiled=True,
    )
    gain_local = jnp.sum(d_normed * normalized, axis=(0, 1))
    gain_sum = lax.psum(gain_local, ("dp", "seq"))
    d_hat = d_normed * norm_gain
    first_mean = jnp.mean(d_hat, axis=-1, keepdims=True)
    second_mean = jnp.mean(d_hat * normalized, axis=-1, keepdims=True)
    input_grad = (inv_std * (d_hat - first_mean - normalized * second_mean)).astype(jnp.bfloat16)
    return (input_grad[None], weight_sum * factor, gain_sum * factor)


MESH = pl.DeviceIdType.MESH
BF = jnp.bfloat16
F32 = jnp.float32
ROWS = 16
PAD = 48
SPLIT = 768


def fused(
    x_ref, do_ref, gain_ref, w_hbm, clip_ref,
    ig_ref, wg_ref, gg_ref,
    w, rn, rp, cn, cp, mk, nz, iv, nb, dos, proj, t1, t2, em, et, bc, g, dn, igs, qn, qp,
    tr, nt, nr, dvr, sx, sy, rx, ry, kx, ky, tx, ty, rtx, rty, fin, u, zr, gp, gr, zg,
    wsem, send, recv,
):
    dp = lax.axis_index("dp")
    s = lax.axis_index("seq")
    z, y = dp // 2, dp % 2
    xx, core = s // 2, s % 2
    half = x_ref.shape[0] // 2
    width = x_ref.shape[1]
    head_dim = width // HEADS
    block = wg_ref.shape[0]
    scaling = head_dim ** (-0.5)
    prev, after = (dp, lax.rem(s + 3, 4)), (dp, lax.rem(s + 1, 4))
    has_prev, has_next = s > 0, s < 3
    core_dev = (dp, xx * 2 + (1 - core))
    x_dev = (dp, (1 - xx) * 2 + core)
    y_dev = (z * 2 + (1 - y), s)
    z_devs = [(lax.rem(z + d, 4) * 2 + y, s) for d in (1, 2, 3)]

    loads = [
        pltpu.make_async_copy(w_hbm.at[:, pl.ds(j * width, width)], w.at[j], wsem.at[j])
        for j in range(3)
    ]
    for load in loads:
        load.start()

    barrier = pltpu.get_barrier_semaphore()
    for dev in [core_dev, x_dev, y_dev, (dp, 3 - s)] + z_devs:
        pl.semaphore_signal(barrier, inc=1, device_id=dev, device_id_type=MESH)
    pl.semaphore_wait(barrier, 7)

    def remote(index, src, dst, dev):
        return pltpu.make_async_remote_copy(
            src_ref=src, dst_ref=dst, send_sem=send.at[index], recv_sem=recv.at[index],
            device_id=dev, device_id_type=MESH,
        )

    lower, upper = pl.ds(0, half), pl.ds(half, half)
    clip_p = remote(4, clip_ref, cn, prev)
    clip_n = remote(5, clip_ref, cp, after)
    x_p = remote(0, x_ref.at[lower], rn.at[0], prev)
    do_p = remote(1, do_ref.at[lower], rn.at[1], prev)
    x_n = remote(2, x_ref.at[upper], rp.at[0], after)
    do_n = remote(3, do_ref.at[upper], rp.at[1], after)
    to_prev, to_next = [clip_p, x_p, do_p], [clip_n, x_n, do_n]

    @pl.when(has_prev)
    def _():
        for copy in to_prev:
            copy.start()

    @pl.when(has_next)
    def _():
        for copy in to_next:
            copy.start()

    @pl.when(s == 0)
    def _():
        rp[...] = jnp.zeros_like(rp)
        cp[...] = jnp.full_like(cp, -1.0)

    @pl.when(s == 3)
    def _():
        rn[...] = jnp.zeros_like(rn)
        cn[...] = jnp.full_like(cn, -1.0)

    row = lax.broadcasted_iota(jnp.int32, em.shape, 0)
    col = lax.broadcasted_iota(jnp.int32, em.shape, 1) * head_dim
    em[...] = jnp.where((row >= col) & (row < col + head_dim), 1.0, 0.0).astype(BF)
    row = lax.broadcasted_iota(jnp.int32, et.shape, 0) * head_dim
    col = lax.broadcasted_iota(jnp.int32, et.shape, 1)
    et[...] = jnp.where((col >= row) & (col < row + head_dim), 1.0, 0.0).astype(BF)
    tr[pl.ds(width, 8), :] = jnp.zeros((8, tr.shape[1]), F32)

    @pl.when(has_next)
    def _():
        clip_p.wait_recv()
        x_p.wait_recv()

    @pl.when(has_prev)
    def _():
        clip_n.wait_recv()
        x_n.wait_recv()

    own_clip = clip_ref[...]
    mk[0] = jnp.where(own_clip == cp[...], 1.0, 0.0)
    mk[1] = jnp.where(own_clip == cn[...], 1.0, 0.0)

    def masks(shape):
        before = jnp.broadcast_to(mk[0, 0:1, 0:1], shape) > 0.5
        later = jnp.broadcast_to(mk[1, 0:1, 0:1], shape) > 0.5
        return before, later

    def pick(own, index, r):
        before, later = masks((ROWS, width))
        lo = own[pl.ds(r, ROWS), :].astype(F32)
        hi = own[pl.ds(half + r, ROWS), :].astype(F32)
        from_next = rn[index, pl.ds(r, ROWS), :].astype(F32)
        from_prev = rp[index, pl.ds(r, ROWS), :].astype(F32)
        first = jnp.where(before, hi, lo)
        second = jnp.where(later, from_next, jnp.where(before, from_prev, hi))
        return first, second

    chunks = half // ROWS

    def norm_rows(c, carry):
        r = pl.multiple_of(c * ROWS, ROWS)
        for base, rows in zip((0, half), pick(x_ref, 0, r)):
            at = pl.ds(base + r, ROWS)
            centered = rows - jnp.mean(rows, axis=-1, keepdims=True)
            inv = lax.rsqrt(jnp.mean(centered * centered, axis=-1, keepdims=True) + epsilon)
            normalized = centered * inv
            nz[at, :] = normalized
            iv[at, :] = jnp.broadcast_to(inv, (ROWS, 128))
            nb[at, :] = (normalized * gain_ref[...]).astype(BF)
        return carry

    lax.fori_loop(0, chunks, norm_rows, 0)

    for j in range(3):
        loads[j].wait()

    def project(j, carry):
        proj[j] = jnp.dot(nb[...], w[j], preferred_element_type=F32).astype(BF)
        return carry

    lax.fori_loop(0, 3, project, 0)

    tr[pl.ds(0, width), :] = jnp.transpose(nb[...].astype(F32))
    for i in range(32):
        nt[i % 2, (i // 2) % 2 * 2 + (i // 4) % 2, pl.ds(i // 8 * PAD, PAD), :] = tr[
            pl.ds(i * block, PAD), :
        ].astype(BF)
    nt_copy = remote(6, nt.at[1 - core], nr, core_dev)
    nt_copy.start()

    @pl.when(has_next)
    def _():
        do_p.wait_recv()

    @pl.when(has_prev)
    def _():
        do_n.wait_recv()

    def products(c, carry):
        r = pl.multiple_of(c * ROWS, ROWS)
        a, b = pl.ds(r, ROWS), pl.ds(half + r, ROWS)
        do_a, do_b = pick(do_ref, 1, r)
        dos[a, :] = do_a.astype(BF)
        dos[b, :] = do_b.astype(BF)
        kd = proj[1, a, :].astype(F32) - proj[1, b, :].astype(F32)
        vd = proj[2, a, :].astype(F32) - proj[2, b, :].astype(F32)
        t1[a, :] = (proj[0, a, :].astype(F32) * kd).astype(BF)
        t1[b, :] = (proj[0, b, :].astype(F32) * -kd).astype(BF)
        t2[a, :] = (do_a * vd).astype(BF)
        t2[b, :] = (do_b * -vd).astype(BF)
        return carry

    lax.fori_loop(0, chunks, products, 0)

    sd = jnp.dot(t1[...], em[...], preferred_element_type=F32) * scaling
    dd = jnp.dot(t2[...], em[...], preferred_element_type=F32)
    before, later = masks(sd.shape)
    paired = before | later
    own_p = jnp.where(paired, 1.0 / (1.0 + jnp.exp(-sd)), 1.0)
    other_p = jnp.where(paired, 1.0 / (1.0 + jnp.exp(sd)), 0.0)
    ds = own_p * other_p * dd * scaling
    for j, small in enumerate((own_p, other_p, ds)):
        bc[j] = jnp.dot(small.astype(BF), et[...], preferred_element_type=F32).astype(BF)

    def value_rows(c, carry):
        r = pl.multiple_of(c * ROWS, ROWS)
        a, b = pl.ds(r, ROWS), pl.ds(half + r, ROWS)
        do_a, do_b = dos[a, :].astype(F32), dos[b, :].astype(F32)
        g[2, a, :] = (bc[0, a, :].astype(F32) * do_a + bc[1, b, :].astype(F32) * do_b).astype(BF)
        g[2, b, :] = (bc[0, b, :].astype(F32) * do_b + bc[1, a, :].astype(F32) * do_a).astype(BF)
        return carry

    lax.fori_loop(0, chunks, value_rows, 0)
    dv_copy = remote(7, g.at[2], dvr, core_dev)
    dv_copy.start()

    def grad_rows(c, carry):
        r = pl.multiple_of(c * ROWS, ROWS)
        a, b = pl.ds(r, ROWS), pl.ds(half + r, ROWS)
        ds_a, ds_b = bc[2, a, :].astype(F32), bc[2, b, :].astype(F32)
        kd = proj[1, a, :].astype(F32) - proj[1, b, :].astype(F32)
        g[0, a, :] = (ds_a * kd).astype(BF)
        g[0, b, :] = (ds_b * -kd).astype(BF)
        dk = ds_a * proj[0, a, :].astype(F32) - ds_b * proj[0, b, :].astype(F32)
        g[1, a, :] = dk.astype(BF)
        g[1, b, :] = (-dk).astype(BF)
        return carry

    lax.fori_loop(0, chunks, grad_rows, 0)

    nt_copy.wait_recv()
    dv_copy.wait_recv()

    def term(group, cols):
        return jnp.dot(nt[core, group], g[2, :, cols], preferred_element_type=F32) + jnp.dot(
            nr[group], dvr[:, cols], preferred_element_type=F32
        )

    cols_y, cols_x = pl.ds(0, SPLIT), pl.ds(SPLIT, width - SPLIT)

    def send_terms(k, carry):
        sx[k] = term((1 - xx) * 2 + k, cols_x).astype(BF)
        sy[k] = term(k * 2 + (1 - y), cols_y).astype(BF)
        return carry

    lax.fori_loop(0, 2, send_terms, 0)
    x_first = remote(10, sx, rx, x_dev)
    y_first = remote(11, sy, ry, y_dev)
    x_first.start()
    y_first.start()

    def back(j, carry):
        part = lax.dot_general(
            g[j], w[j], (((1,), (1,)), ((), ())), preferred_element_type=F32
        )
        dn[...] = dn[...] + part
        return carry

    dn[...] = jnp.zeros_like(dn)
    lax.fori_loop(0, 3, back, 0)

    def input_rows(c, acc):
        r = pl.multiple_of(c * ROWS, ROWS)
        at = pl.ds(r, ROWS)
        normalized, d_normed = nz[at, :], dn[at, :]
        prod = d_normed * normalized
        d_hat = d_normed * gain_ref[...]
        first = jnp.mean(d_hat, axis=-1, keepdims=True)
        second = jnp.mean(d_hat * normalized, axis=-1, keepdims=True)
        result = iv[at, 0:1] * (d_hat - first - normalized * second)
        igs[at, :] = result.astype(BF)
        return acc + (prod[0:8] + prod[8:16])

    gp[0] = lax.fori_loop(0, 2 * chunks, input_rows, jnp.zeros((8, width), F32))

    ig_p = remote(8, igs.at[upper], qn, prev)
    ig_n = remote(9, igs.at[upper], qp, after)

    @pl.when(has_prev)
    def _():
        ig_p.start()

    @pl.when(has_next)
    def _():
        ig_n.start()

    @pl.when(s == 0)
    def _():
        qp[...] = jnp.zeros_like(qp)

    @pl.when(s == 3)
    def _():
        qn[...] = jnp.zeros_like(qn)

    gain_core = remote(17, gp.at[0], gr.at[0], core_dev)
    gain_core.start()

    def keep_terms(k, carry):
        kx[k] = term(xx * 2 + k, cols_x)
        ky[k] = term(k * 2 + y, cols_y)
        return carry

    lax.fori_loop(0, 2, keep_terms, 0)

    gain_core.wait_recv()
    gp[1] = gp[0] + gr[0]
    gain_x = remote(18, gp.at[1], gr.at[1], x_dev)
    gain_x.start()

    y_first.wait_recv()
    tx[...] = (ky[1 - xx] + ry[1 - xx].astype(F32)).astype(BF)
    x_second = remote(12, tx, rtx, x_dev)
    x_second.start()
    x_first.wait_recv()
    ty[...] = (kx[1 - y] + rx[1 - y].astype(F32)).astype(BF)
    y_second = remote(13, ty, rty, y_dev)
    y_second.start()

    gain_x.wait_recv()
    gp[2] = gp[1] + gr[1]
    gain_y = remote(19, gp.at[2], gr.at[2], y_dev)
    gain_y.start()

    fin[:, cols_y] = ky[xx] + ry[xx].astype(F32)
    fin[:, cols_x] = kx[y] + rx[y].astype(F32)

    gain_y.wait_recv()
    zg[z] = gp[2] + gr[2]
    gain_z = [remote(20 + d, zg.at[z], zg.at[z], z_devs[d]) for d in range(3)]
    for copy in gain_z:
        copy.start()

    @pl.when(has_next)
    def _():
        ig_p.wait_recv()

    @pl.when(has_prev)
    def _():
        ig_n.wait_recv()

    def output_rows(c, carry):
        r = pl.multiple_of(c * ROWS, ROWS)
        a, b = pl.ds(r, ROWS), pl.ds(half + r, ROWS)
        prior, later_too = masks((ROWS, width))
        first, second = igs[a, :].astype(F32), igs[b, :].astype(F32)
        ig_ref[a, :] = jnp.where(prior, qp[a, :].astype(F32), first).astype(BF)
        ig_ref[b, :] = jnp.where(
            prior, first, jnp.where(later_too, qn[a, :].astype(F32), second)
        ).astype(BF)
        return carry

    lax.fori_loop(0, chunks, output_rows, 0)

    x_second.wait_recv()
    fin[:, cols_y] = fin[:, cols_y] + rtx[...].astype(F32)
    y_second.wait_recv()
    fin[:, cols_x] = fin[:, cols_x] + rty[...].astype(F32)
    for k in range(4):
        u[k] = fin[pl.ds(k * PAD, PAD), :].astype(BF)
    z_copies = [
        remote(14 + d, u.at[lax.rem(z + d + 1, 4)], zr.at[d], z_devs[d]) for d in range(3)
    ]
    for copy in z_copies:
        copy.start()

    factor = (x_ref.shape[0] * 32) ** (-0.5)
    for copy in gain_z:
        copy.wait_recv()
    total = (zg[0] + zg[1]) + (zg[2] + zg[3])
    gg_ref[...] = jnp.sum(total, axis=0, keepdims=True) * factor

    for copy in z_copies:
        copy.wait_recv()
    own = fin[pl.ds(pl.multiple_of(z * PAD, PAD), PAD), :]
    summed = own + zr[0].astype(F32) + zr[1].astype(F32) + zr[2].astype(F32)
    wg_ref[...] = summed[0:block] * factor

    @pl.when(has_prev)
    def _():
        for copy in to_prev + [ig_p]:
            copy.wait_send()

    @pl.when(has_next)
    def _():
        for copy in to_next + [ig_n]:
            copy.wait_send()

    sent = [nt_copy, dv_copy, x_first, y_first, x_second, y_second, gain_core, gain_x, gain_y]
    for copy in sent + gain_z + z_copies:
        copy.wait_send()


def paired_shards(block_input, norm_gain, qkv_weight, frame_clip, out_grad):
    tokens, width = block_input.shape[2:]
    half = tokens // 2
    block = width // 32
    clip = jnp.broadcast_to(frame_clip.astype(F32), (8, 128))
    vmem = pl.BlockSpec(memory_space=pltpu.VMEM)
    rest = width - SPLIT
    group = 4 * PAD

    def buf(*shape):
        return pltpu.VMEM(shape, BF)

    def wide(*shape):
        return pltpu.VMEM(shape, F32)

    scratch = [
        buf(3, width, width), buf(2, half, width), buf(2, half, width),
        wide(8, 128), wide(8, 128), wide(2, 8, 128),
        wide(tokens, width), wide(tokens, 128), buf(tokens, width), buf(tokens, width),
        buf(3, tokens, width), buf(tokens, width), buf(tokens, width),
        buf(width, 128), buf(128, width), buf(3, tokens, width), buf(3, tokens, width),
        wide(tokens, width), buf(tokens, width), buf(half, width), buf(half, width),
        wide(width + 8, tokens), buf(2, 4, group, tokens), buf(4, group, tokens),
        buf(tokens, width),
        buf(2, group, rest), buf(2, group, SPLIT), buf(2, group, rest), buf(2, group, SPLIT),
        wide(2, group, rest), wide(2, group, SPLIT),
        buf(group, SPLIT), buf(group, rest), buf(group, SPLIT), buf(group, rest),
        wide(group, width), buf(4, PAD, width), buf(3, PAD, width),
        wide(3, 8, width), wide(3, 8, width), wide(4, 8, width),
        pltpu.SemaphoreType.DMA((3,)),
        pltpu.SemaphoreType.DMA((23,)), pltpu.SemaphoreType.DMA((23,)),
    ]
    input_grad, weight_grad, gain_grad = pl.pallas_call(
        fused,
        out_shape=(
            jax.ShapeDtypeStruct((tokens, width), BF),
            jax.ShapeDtypeStruct((block, width), F32),
            jax.ShapeDtypeStruct((1, width), F32),
        ),
        in_specs=[vmem, vmem, vmem, pl.BlockSpec(memory_space=pl.ANY), vmem],
        out_specs=(vmem, vmem, vmem),
        scratch_shapes=scratch,
        compiler_params=pltpu.CompilerParams(
            collective_id=0, has_side_effects=True, vmem_limit_bytes=56 * 1024 * 1024
        ),
        cost_estimate=pl.CostEstimate(
            flops=8_000_000_000, bytes_accessed=16_000_000, transcendentals=100_000
        ),
    )(block_input[0, 0], out_grad[0, 0], norm_gain[None], qkv_weight, clip)
    return input_grad[None, None], weight_grad, gain_grad[0]


def solution(mesh):
    placed = (P("dp", "seq", None, None), P(), P(), P("dp", "seq"), P("dp", "seq", None, None))

    def whole(block_input, *others):
        small = mesh.shape["dp"] == 8 and mesh.shape["seq"] == 4 and block_input.shape[1] == 4
        return jax.shard_map(
            paired_shards if small else shards,
            mesh=mesh,
            in_specs=placed,
            out_specs=(P("dp", "seq", None, None), P(("dp", "seq"), None), P()),
            check_vma=False,
        )(block_input, *others)

    return whole
```

```python
import jax
import jax.numpy as jnp
from jax import lax
from jax.experimental import pallas as pl
from jax.experimental.pallas import tpu as pltpu
from jax.sharding import PartitionSpec as P

HEADS = 16


epsilon = 1e-06


def attention_grad(projected, incoming, same_clip):
    frames_all, positions, triple = projected.shape
    width = triple // 3
    head_dim = width // HEADS
    blocks = projected.reshape(frames_all, positions, 3, HEADS, head_dim)
    query_part = blocks[:, :, 0]
    key_part = blocks[:, :, 1]
    value_part = blocks[:, :, 2]
    outgrad = incoming.reshape(frames_all, positions, HEADS, head_dim)
    scaling = head_dim ** (-0.5)
    scores = (
        jnp.einsum("fphd,gphd->phfg", query_part, key_part, preferred_element_type=jnp.float32)
        * scaling
    )
    largest = jnp.max(jnp.where(same_clip, scores, -jnp.inf), axis=-1, keepdims=True)
    powers = jnp.where(same_clip, jnp.exp(scores - largest), 0.0)
    softmaxed = powers / jnp.sum(powers, axis=-1, keepdims=True)
    rounded_probs = softmaxed.astype(jnp.bfloat16)
    d_value = jnp.einsum(
        "phfg,fphd->gphd", rounded_probs, outgrad, preferred_element_type=jnp.float32
    )
    d_probs = jnp.einsum("fphd,gphd->phfg", outgrad, value_part, preferred_element_type=jnp.float32)
    row_dot = jnp.sum(softmaxed * d_probs, axis=-1, keepdims=True)
    d_scores = (softmaxed * (d_probs - row_dot) * scaling).astype(jnp.bfloat16)
    d_query = jnp.einsum("phfg,gphd->fphd", d_scores, key_part, preferred_element_type=jnp.float32)
    d_key = jnp.einsum("phfg,fphd->gphd", d_scores, query_part, preferred_element_type=jnp.float32)
    stacked = jnp.stack([d_query, d_key, d_value], axis=2)
    return stacked.reshape(frames_all, positions, triple).astype(jnp.bfloat16)


def transpose_product(grad_rows, qkv_weight):
    return lax.dot_general(
        grad_rows, qkv_weight, (((1,), (1,)), ((), ())), preferred_element_type=jnp.float32
    )


def shards(block_input, norm_gain, qkv_weight, frame_clip, out_grad):
    frames_dev = block_input.shape[1]
    patches = block_input.shape[2]
    width = block_input.shape[3]
    seq_count = lax.axis_size("seq")
    group_count = lax.axis_size("dp")
    local_pos = patches // seq_count
    factor = (frames_dev * patches * seq_count * group_count) ** (-0.5)
    inputs_f = block_input[0].astype(jnp.float32)
    centered = inputs_f - jnp.mean(inputs_f, axis=-1, keepdims=True)
    inv_std = lax.rsqrt(jnp.mean(centered * centered, axis=-1, keepdims=True) + epsilon)
    normalized = centered * inv_std
    normed = (normalized * norm_gain).astype(jnp.bfloat16)
    clip_ids = lax.all_gather(frame_clip, "seq", axis=1, tiled=True)[0]
    same_clip = clip_ids[:, None] == clip_ids[None, :]
    grad_split = out_grad[0].reshape(frames_dev, seq_count, local_pos, width)
    projected = jnp.dot(normed.reshape(-1, width), qkv_weight, preferred_element_type=jnp.float32)
    projected = projected.astype(jnp.bfloat16).reshape(frames_dev, seq_count, local_pos, 3 * width)
    moved_proj = lax.all_to_all(projected, "seq", split_axis=1, concat_axis=0, tiled=True)
    incoming = lax.all_to_all(grad_split, "seq", split_axis=1, concat_axis=0, tiled=True)
    grads_frames = attention_grad(moved_proj[:, 0], incoming[:, 0], same_clip)[:, None]
    grads_qkv = lax.all_to_all(grads_frames, "seq", split_axis=0, concat_axis=1, tiled=True)
    rows_x = normed.reshape(-1, width)
    rows_g = grads_qkv.reshape(-1, 3 * width)
    d_normed = transpose_product(rows_g, qkv_weight).reshape(frames_dev, patches, width)
    value_rows = rows_g[:, 2 * width :]
    weight_sum = lax.psum_scatter(
        lax.dot_general(
            rows_x, value_rows, (((0,), (0,)), ((), ())), preferred_element_type=jnp.float32
        ),
        ("dp", "seq"),
        scatter_dimension=0,
        tiled=True,
    )
    gain_local = jnp.sum(d_normed * normalized, axis=(0, 1))
    gain_sum = lax.psum(gain_local, ("dp", "seq"))
    d_hat = d_normed * norm_gain
    first_mean = jnp.mean(d_hat, axis=-1, keepdims=True)
    second_mean = jnp.mean(d_hat * normalized, axis=-1, keepdims=True)
    input_grad = (inv_std * (d_hat - first_mean - normalized * second_mean)).astype(jnp.bfloat16)
    return (input_grad[None], weight_sum * factor, gain_sum * factor)


MESH = pl.DeviceIdType.MESH
BF = jnp.bfloat16
F32 = jnp.float32
ROWS = 16
PAD = 48
SPLIT = 896
PARTS_Y = ((0, 384), (384, 256), (640, 256))
PARTS_X = ((0, 256), (256, 128), (384, 128))
CHUNKS = range(3)


def fused(
    x_ref, do_ref, gain_ref, w_hbm, clip_ref,
    ig_ref, wg_ref, gg_ref,
    gn, cl, w, rn, rp, cn, cp, mk, nz, iv, nb, dos, proj, t1, t2, em, et, bc, g, dn, igs, qn, qp,
    tr, nt, nr, dvr, sx, sy, rx, ry, kx, ky, tx, ty, rtx, rty, fin, u, zr, gp, gr, zg,
    wsem, send, recv,
):
    dp = lax.axis_index("dp")
    s = lax.axis_index("seq")
    z, y = dp // 2, dp % 2
    xx, core = s // 2, s % 2
    half = x_ref.shape[0] // 2
    width = x_ref.shape[1]
    head_dim = width // HEADS
    block = wg_ref.shape[0]
    scaling = head_dim ** (-0.5)
    prev, after = (dp, lax.rem(s + 3, 4)), (dp, lax.rem(s + 1, 4))
    has_prev, has_next = s > 0, s < 3
    core_dev = (dp, xx * 2 + (1 - core))
    x_dev = (dp, (1 - xx) * 2 + core)
    y_dev = (z * 2 + (1 - y), s)
    z_devs = [(lax.rem(z + d, 4) * 2 + y, s) for d in (1, 2, 3)]

    loads = [
        pltpu.make_async_copy(w_hbm.at[:, pl.ds(j * width, width)], w.at[j], wsem.at[j])
        for j in range(3)
    ]
    for load in loads:
        load.start()

    gn[...] = gain_ref[...].reshape(1, width)
    cl[...] = jnp.full(cl.shape, clip_ref[0, 0], jnp.int32)

    barrier = pltpu.get_barrier_semaphore()
    for dev in [core_dev, x_dev, y_dev, (dp, 3 - s)] + z_devs:
        pl.semaphore_signal(barrier, inc=1, device_id=dev, device_id_type=MESH)
    pl.semaphore_wait(barrier, 7)

    def remote(index, src, dst, dev):
        return pltpu.make_async_remote_copy(
            src_ref=src, dst_ref=dst, send_sem=send.at[index], recv_sem=recv.at[index],
            device_id=dev, device_id_type=MESH,
        )

    lower, upper = pl.ds(0, half), pl.ds(half, half)
    clip_p = remote(4, cl, cn, prev)
    clip_n = remote(5, cl, cp, after)
    x_p = remote(0, x_ref.at[lower], rn.at[0], prev)
    do_p = remote(1, do_ref.at[lower], rn.at[1], prev)
    x_n = remote(2, x_ref.at[upper], rp.at[0], after)
    do_n = remote(3, do_ref.at[upper], rp.at[1], after)
    to_prev, to_next = [clip_p, x_p, do_p], [clip_n, x_n, do_n]

    @pl.when(has_prev)
    def _():
        for copy in to_prev:
            copy.start()

    @pl.when(has_next)
    def _():
        for copy in to_next:
            copy.start()

    @pl.when(s == 0)
    def _():
        rp[...] = jnp.zeros_like(rp)
        cp[...] = jnp.full_like(cp, -1)

    @pl.when(s == 3)
    def _():
        rn[...] = jnp.zeros_like(rn)
        cn[...] = jnp.full_like(cn, -1)

    row = lax.broadcasted_iota(jnp.int32, em.shape, 0)
    col = lax.broadcasted_iota(jnp.int32, em.shape, 1) * head_dim
    em[...] = jnp.where((row >= col) & (row < col + head_dim), 1.0, 0.0).astype(BF)
    row = lax.broadcasted_iota(jnp.int32, et.shape, 0) * head_dim
    col = lax.broadcasted_iota(jnp.int32, et.shape, 1)
    et[...] = jnp.where((col >= row) & (col < row + head_dim), 1.0, 0.0).astype(BF)
    tr[pl.ds(width, 8), :] = jnp.zeros((8, tr.shape[1]), F32)

    @pl.when(has_next)
    def _():
        clip_p.wait_recv()

    @pl.when(has_prev)
    def _():
        clip_n.wait_recv()

    own_clip = cl[...]
    mk[0] = jnp.where(own_clip == cp[...], 1.0, 0.0)
    mk[1] = jnp.where(own_clip == cn[...], 1.0, 0.0)

    def masks(shape):
        before = jnp.broadcast_to(mk[0, 0:1, 0:1], shape) > 0.5
        later = jnp.broadcast_to(mk[1, 0:1, 0:1], shape) > 0.5
        return before, later

    def pick_first(own, index, r):
        before, _ = masks((ROWS, width))
        lo = own[pl.ds(r, ROWS), :].astype(F32)
        hi = own[pl.ds(half + r, ROWS), :].astype(F32)
        return jnp.where(before, hi, lo)

    def pick_second(own, index, r):
        before, later = masks((ROWS, width))
        hi = own[pl.ds(half + r, ROWS), :].astype(F32)
        from_next = rn[index, pl.ds(r, ROWS), :].astype(F32)
        from_prev = rp[index, pl.ds(r, ROWS), :].astype(F32)
        return jnp.where(later, from_next, jnp.where(before, from_prev, hi))

    chunks = half // ROWS

    def norm_half(base, pick):
        def norm_rows(c, carry):
            r = pl.multiple_of(c * ROWS, ROWS)
            rows = pick(x_ref, 0, r)
            at = pl.ds(base + r, ROWS)
            centered = rows - jnp.mean(rows, axis=-1, keepdims=True)
            inv = lax.rsqrt(jnp.mean(centered * centered, axis=-1, keepdims=True) + epsilon)
            normalized = centered * inv
            nz[at, :] = normalized
            iv[at, :] = jnp.broadcast_to(inv, (ROWS, 128))
            nb[at, :] = (normalized * gn[...]).astype(BF)
            return carry

        lax.fori_loop(0, chunks, norm_rows, 0, unroll=2)

    def project_half(base):
        rows = pl.ds(base, half)

        def project(j, carry):
            proj[j, rows, :] = jnp.dot(nb[rows, :], w[j], preferred_element_type=F32).astype(BF)
            return carry

        lax.fori_loop(0, 3, project, 0)

    def turn_half(base):
        rows = pl.ds(base, half)
        tr[pl.ds(0, width), :] = jnp.transpose(nb[rows, :].astype(F32))
        for i in range(32):
            nt[i % 2, (i // 2) % 2 * 2 + (i // 4) % 2, pl.ds(i // 8 * PAD, PAD), rows] = tr[
                pl.ds(i * block, PAD), :
            ].astype(BF)

    norm_half(0, pick_first)
    turn_half(0)
    for j in range(3):
        loads[j].wait()
    project_half(0)

    @pl.when(has_next)
    def _():
        x_p.wait_recv()

    @pl.when(has_prev)
    def _():
        x_n.wait_recv()

    norm_half(half, pick_second)
    project_half(half)
    turn_half(half)
    nt_copy = remote(6, nt.at[1 - core], nr, core_dev)
    nt_copy.start()

    @pl.when(has_next)
    def _():
        do_p.wait_recv()

    @pl.when(has_prev)
    def _():
        do_n.wait_recv()

    def products(c, carry):
        r = pl.multiple_of(c * ROWS, ROWS)
        a, b = pl.ds(r, ROWS), pl.ds(half + r, ROWS)
        do_a, do_b = pick_first(do_ref, 1, r), pick_second(do_ref, 1, r)
        dos[a, :] = do_a.astype(BF)
        dos[b, :] = do_b.astype(BF)
        kd = proj[1, a, :].astype(F32) - proj[1, b, :].astype(F32)
        vd = proj[2, a, :].astype(F32) - proj[2, b, :].astype(F32)
        t1[a, :] = (proj[0, a, :].astype(F32) * kd).astype(BF)
        t1[b, :] = (proj[0, b, :].astype(F32) * -kd).astype(BF)
        t2[a, :] = (do_a * vd).astype(BF)
        t2[b, :] = (do_b * -vd).astype(BF)
        return carry

    lax.fori_loop(0, chunks, products, 0)

    sd = jnp.dot(t1[...], em[...], preferred_element_type=F32) * scaling
    dd = jnp.dot(t2[...], em[...], preferred_element_type=F32)
    before, later = masks(sd.shape)
    paired = before | later
    own_p = jnp.where(paired, 1.0 / (1.0 + jnp.exp(-sd)), 1.0)
    other_p = jnp.where(paired, 1.0 / (1.0 + jnp.exp(sd)), 0.0)
    ds = own_p * other_p * dd * scaling
    for j, small in enumerate((own_p, other_p, ds)):
        bc[j] = jnp.dot(small.astype(BF), et[...], preferred_element_type=F32).astype(BF)

    def value_rows(c, carry):
        r = pl.multiple_of(c * ROWS, ROWS)
        a, b = pl.ds(r, ROWS), pl.ds(half + r, ROWS)
        do_a, do_b = dos[a, :].astype(F32), dos[b, :].astype(F32)
        g[2, a, :] = (bc[0, a, :].astype(F32) * do_a + bc[1, b, :].astype(F32) * do_b).astype(BF)
        g[2, b, :] = (bc[0, b, :].astype(F32) * do_b + bc[1, a, :].astype(F32) * do_a).astype(BF)
        return carry

    lax.fori_loop(0, chunks, value_rows, 0)
    dv_copy = remote(7, g.at[2], dvr, core_dev)
    dv_copy.start()

    def grad_rows(c, carry):
        r = pl.multiple_of(c * ROWS, ROWS)
        a, b = pl.ds(r, ROWS), pl.ds(half + r, ROWS)
        ds_a, ds_b = bc[2, a, :].astype(F32), bc[2, b, :].astype(F32)
        kd = proj[1, a, :].astype(F32) - proj[1, b, :].astype(F32)
        g[0, a, :] = (ds_a * kd).astype(BF)
        g[0, b, :] = (ds_b * -kd).astype(BF)
        dk = ds_a * proj[0, a, :].astype(F32) - ds_b * proj[0, b, :].astype(F32)
        g[1, a, :] = dk.astype(BF)
        g[1, b, :] = (-dk).astype(BF)
        return carry

    lax.fori_loop(0, chunks, grad_rows, 0)

    nt_copy.wait_recv()
    dv_copy.wait_recv()

    def term(group, cols):
        return jnp.dot(nt[core, group], g[2, :, cols], preferred_element_type=F32) + jnp.dot(
            nr[group], dvr[:, cols], preferred_element_type=F32
        )

    def in_y(k):
        return pl.ds(*PARTS_Y[k])

    def in_x(k):
        return pl.ds(*PARTS_X[k])

    def from_x(k):
        return pl.ds(SPLIT + PARTS_X[k][0], PARTS_X[k][1])

    x_first, y_first, x_second, y_second = [], [], [], []
    for k in CHUNKS:

        def send_terms(n, carry, k=k):
            sx[n, :, in_x(k)] = term((1 - xx) * 2 + n, from_x(k)).astype(BF)
            sy[n, :, in_y(k)] = term(n * 2 + (1 - y), in_y(k)).astype(BF)
            return carry

        lax.fori_loop(0, 2, send_terms, 0)
        x_first.append(remote(10 + k, sx.at[:, :, in_x(k)], rx.at[:, :, in_x(k)], x_dev))
        y_first.append(remote(13 + k, sy.at[:, :, in_y(k)], ry.at[:, :, in_y(k)], y_dev))
        x_first[k].start()
        y_first[k].start()

    def back(j, carry):
        part = lax.dot_general(
            g[j], w[j], (((1,), (1,)), ((), ())), preferred_element_type=F32
        )
        dn[...] = dn[...] + part
        return carry

    dn[...] = jnp.zeros_like(dn)
    lax.fori_loop(0, 3, back, 0)

    def input_rows(c, acc):
        r = pl.multiple_of(c * ROWS, ROWS)
        at = pl.ds(r, ROWS)
        normalized, d_normed = nz[at, :], dn[at, :]
        prod = d_normed * normalized
        d_hat = d_normed * gn[...]
        first = jnp.mean(d_hat, axis=-1, keepdims=True)
        second = jnp.mean(d_hat * normalized, axis=-1, keepdims=True)
        result = iv[at, 0:1] * (d_hat - first - normalized * second)
        igs[at, :] = result.astype(BF)
        return acc + (prod[0:8] + prod[8:16])

    gp[0] = lax.fori_loop(
        0, 2 * chunks, input_rows, jnp.zeros((8, width), F32), unroll=2
    )

    ig_p = remote(8, igs.at[upper], qn, prev)
    ig_n = remote(9, igs.at[upper], qp, after)

    @pl.when(s == 0)
    def _():
        qp[...] = jnp.zeros_like(qp)

    @pl.when(s == 3)
    def _():
        qn[...] = jnp.zeros_like(qn)

    gain_core = remote(16, gp.at[0], gr.at[0], core_dev)
    gain_core.start()

    def keep_terms(n, carry):
        kx[n] = term(xx * 2 + n, pl.ds(SPLIT, width - SPLIT))
        ky[n] = term(n * 2 + y, pl.ds(0, SPLIT))
        return carry

    lax.fori_loop(0, 2, keep_terms, 0)

    gain_core.wait_recv()
    gp[1] = gp[0] + gr[0]
    gain_x = remote(17, gp.at[1], gr.at[1], x_dev)
    gain_x.start()

    for k in CHUNKS:
        y_first[k].wait_recv()
        tx[:, in_y(k)] = (
            ky[1 - xx, :, in_y(k)] + ry[1 - xx, :, in_y(k)].astype(F32)
        ).astype(BF)
        x_second.append(remote(18 + k, tx.at[:, in_y(k)], rtx.at[:, in_y(k)], x_dev))
        x_second[k].start()
        x_first[k].wait_recv()
        ty[:, in_x(k)] = (
            kx[1 - y, :, in_x(k)] + rx[1 - y, :, in_x(k)].astype(F32)
        ).astype(BF)
        y_second.append(remote(21 + k, ty.at[:, in_x(k)], rty.at[:, in_x(k)], y_dev))
        y_second[k].start()
        fin[:, in_y(k)] = ky[xx, :, in_y(k)] + ry[xx, :, in_y(k)].astype(F32)
        fin[:, from_x(k)] = kx[y, :, in_x(k)] + rx[y, :, in_x(k)].astype(F32)

    @pl.when(has_prev)
    def _():
        ig_p.start()

    @pl.when(has_next)
    def _():
        ig_n.start()

    gain_x.wait_recv()
    gp[2] = gp[1] + gr[1]
    gain_y = remote(24, gp.at[2], gr.at[2], y_dev)
    gain_y.start()

    z_copies = []

    def pass_on(index, cols):
        for n in range(4):
            u[n, :, cols] = fin[pl.ds(n * PAD, PAD), cols].astype(BF)
        for d in range(3):
            z_copies.append(
                remote(
                    index + d, u.at[lax.rem(z + d + 1, 4), :, cols], zr.at[d, :, cols], z_devs[d]
                )
            )
            z_copies[-1].start()

    for k in CHUNKS:
        y_second[k].wait_recv()
        fin[:, from_x(k)] = fin[:, from_x(k)] + rty[:, in_x(k)].astype(F32)
        pass_on(28 + 6 * k, from_x(k))
        x_second[k].wait_recv()
        fin[:, in_y(k)] = fin[:, in_y(k)] + rtx[:, in_y(k)].astype(F32)
        pass_on(31 + 6 * k, in_y(k))

    gain_y.wait_recv()
    zg[z] = gp[2] + gr[2]
    gain_z = [remote(25 + d, zg.at[z], zg.at[z], z_devs[d]) for d in range(3)]
    for copy in gain_z:
        copy.start()

    @pl.when(has_next)
    def _():
        ig_p.wait_recv()

    @pl.when(has_prev)
    def _():
        ig_n.wait_recv()

    def output_rows(c, carry):
        r = pl.multiple_of(c * ROWS, ROWS)
        a, b = pl.ds(r, ROWS), pl.ds(half + r, ROWS)
        prior, later_too = masks((ROWS, width))
        first, second = igs[a, :].astype(F32), igs[b, :].astype(F32)
        ig_ref[a, :] = jnp.where(prior, qp[a, :].astype(F32), first).astype(BF)
        ig_ref[b, :] = jnp.where(
            prior, first, jnp.where(later_too, qn[a, :].astype(F32), second)
        ).astype(BF)
        return carry

    lax.fori_loop(0, chunks, output_rows, 0)

    factor = (x_ref.shape[0] * 32) ** (-0.5)
    for copy in gain_z:
        copy.wait_recv()
    total = (zg[0] + zg[1]) + (zg[2] + zg[3])
    gg_ref[...] = jnp.sum(total, axis=0) * factor

    for copy in z_copies:
        copy.wait_recv()
    own = fin[pl.ds(pl.multiple_of(z * PAD, PAD), PAD), :]
    summed = own + zr[0].astype(F32) + zr[1].astype(F32) + zr[2].astype(F32)
    wg_ref[...] = summed[0:block] * factor

    @pl.when(has_prev)
    def _():
        for copy in to_prev + [ig_p]:
            copy.wait_send()

    @pl.when(has_next)
    def _():
        for copy in to_next + [ig_n]:
            copy.wait_send()

    sent = [nt_copy, dv_copy, gain_core, gain_x, gain_y] + x_first + y_first
    for copy in sent + x_second + y_second + gain_z + z_copies:
        copy.wait_send()


def settle(a, b, c, a_out, b_out, c_out, sem):
    copies = [
        pltpu.make_async_copy(src, dst, sem.at[i])
        for i, (src, dst) in enumerate(((a, a_out), (b, b_out), (c, c_out)))
    ]
    for copy in copies:
        copy.start()
    for copy in copies:
        copy.wait()


def paired_shards(block_input, norm_gain, qkv_weight, frame_clip, out_grad):
    tokens, width = block_input.shape[2:]
    half = tokens // 2
    block = width // 32
    smem = pl.BlockSpec(memory_space=pltpu.SMEM)
    vmem = pl.BlockSpec(memory_space=pltpu.VMEM)
    rest = width - SPLIT
    group = 4 * PAD

    def buf(*shape):
        return pltpu.VMEM(shape, BF)

    def ids(*shape):
        return pltpu.VMEM(shape, jnp.int32)

    def wide(*shape):
        return pltpu.VMEM(shape, F32)

    scratch = [
        wide(1, width), ids(8, 128), buf(3, width, width), buf(2, half, width), buf(2, half, width),
        ids(8, 128), ids(8, 128), wide(2, 8, 128),
        wide(tokens, width), wide(tokens, 128), buf(tokens, width), buf(tokens, width),
        buf(3, tokens, width), buf(tokens, width), buf(tokens, width),
        buf(width, 128), buf(128, width), buf(3, tokens, width), buf(3, tokens, width),
        wide(tokens, width), buf(tokens, width), buf(half, width), buf(half, width),
        wide(width + 8, half), buf(2, 4, group, tokens), buf(4, group, tokens),
        buf(tokens, width),
        buf(2, group, rest), buf(2, group, SPLIT), buf(2, group, rest), buf(2, group, SPLIT),
        wide(2, group, rest), wide(2, group, SPLIT),
        buf(group, SPLIT), buf(group, rest), buf(group, SPLIT), buf(group, rest),
        wide(group, width), buf(4, PAD, width), buf(3, PAD, width),
        wide(3, 8, width), wide(3, 8, width), wide(4, 8, width),
        pltpu.SemaphoreType.DMA((3,)),
        pltpu.SemaphoreType.DMA((46,)), pltpu.SemaphoreType.DMA((46,)),
    ]
    results = pl.pallas_call(
        fused,
        out_shape=(
            jax.ShapeDtypeStruct((tokens, width), BF),
            jax.ShapeDtypeStruct((block, width), F32),
            jax.ShapeDtypeStruct((width,), F32),
        ),
        in_specs=[vmem, vmem, vmem, pl.BlockSpec(memory_space=pl.ANY), smem],
        out_specs=(vmem, vmem, vmem),
        scratch_shapes=scratch,
        compiler_params=pltpu.CompilerParams(
            collective_id=0, has_side_effects=True, vmem_limit_bytes=56 * 1024 * 1024
        ),
        cost_estimate=pl.CostEstimate(
            flops=8_000_000_000, bytes_accessed=16_000_000, transcendentals=100_000
        ),
    )(block_input[0, 0], out_grad[0, 0], norm_gain, qkv_weight, frame_clip)
    any_place = pl.BlockSpec(memory_space=pl.ANY)
    input_grad, weight_grad, gain_grad = pl.pallas_call(
        settle,
        out_shape=tuple(jax.ShapeDtypeStruct(r.shape, r.dtype) for r in results),
        in_specs=[any_place] * 3,
        out_specs=(any_place,) * 3,
        scratch_shapes=[pltpu.SemaphoreType.DMA((3,))],
    )(*results)
    return input_grad[None, None], weight_grad, gain_grad


def solution(mesh):
    placed = (P("dp", "seq", None, None), P(), P(), P("dp", "seq"), P("dp", "seq", None, None))

    def whole(block_input, *others):
        small = mesh.shape["dp"] == 8 and mesh.shape["seq"] == 4 and block_input.shape[1] == 4
        return jax.shard_map(
            paired_shards if small else shards,
            mesh=mesh,
            in_specs=placed,
            out_specs=(P("dp", "seq", None, None), P(("dp", "seq"), None), P()),
            check_vma=False,
        )(block_input, *others)

    return whole
```

```python
import jax
import jax.numpy as jnp
from jax import lax
from jax.experimental import pallas as pl
from jax.experimental.pallas import tpu as pltpu
from jax.sharding import PartitionSpec as P

HEADS = 16


epsilon = 1e-06


def attention_grad(projected, incoming, same_clip):
    frames_all, positions, triple = projected.shape
    width = triple // 3
    head_dim = width // HEADS
    blocks = projected.reshape(frames_all, positions, 3, HEADS, head_dim)
    query_part = blocks[:, :, 0]
    key_part = blocks[:, :, 1]
    value_part = blocks[:, :, 2]
    outgrad = incoming.reshape(frames_all, positions, HEADS, head_dim)
    scaling = head_dim ** (-0.5)
    scores = (
        jnp.einsum("fphd,gphd->phfg", query_part, key_part, preferred_element_type=jnp.float32)
        * scaling
    )
    largest = jnp.max(jnp.where(same_clip, scores, -jnp.inf), axis=-1, keepdims=True)
    powers = jnp.where(same_clip, jnp.exp(scores - largest), 0.0)
    softmaxed = powers / jnp.sum(powers, axis=-1, keepdims=True)
    rounded_probs = softmaxed.astype(jnp.bfloat16)
    d_value = jnp.einsum(
        "phfg,fphd->gphd", rounded_probs, outgrad, preferred_element_type=jnp.float32
    )
    d_probs = jnp.einsum("fphd,gphd->phfg", outgrad, value_part, preferred_element_type=jnp.float32)
    row_dot = jnp.sum(softmaxed * d_probs, axis=-1, keepdims=True)
    d_scores = (softmaxed * (d_probs - row_dot) * scaling).astype(jnp.bfloat16)
    d_query = jnp.einsum("phfg,gphd->fphd", d_scores, key_part, preferred_element_type=jnp.float32)
    d_key = jnp.einsum("phfg,fphd->gphd", d_scores, query_part, preferred_element_type=jnp.float32)
    stacked = jnp.stack([d_query, d_key, d_value], axis=2)
    return stacked.reshape(frames_all, positions, triple).astype(jnp.bfloat16)


def transpose_product(grad_rows, qkv_weight):
    return lax.dot_general(
        grad_rows, qkv_weight, (((1,), (1,)), ((), ())), preferred_element_type=jnp.float32
    )


def shards(block_input, norm_gain, qkv_weight, frame_clip, out_grad):
    frames_dev = block_input.shape[1]
    patches = block_input.shape[2]
    width = block_input.shape[3]
    seq_count = lax.axis_size("seq")
    group_count = lax.axis_size("dp")
    local_pos = patches // seq_count
    factor = (frames_dev * patches * seq_count * group_count) ** (-0.5)
    inputs_f = block_input[0].astype(jnp.float32)
    centered = inputs_f - jnp.mean(inputs_f, axis=-1, keepdims=True)
    inv_std = lax.rsqrt(jnp.mean(centered * centered, axis=-1, keepdims=True) + epsilon)
    normalized = centered * inv_std
    normed = (normalized * norm_gain).astype(jnp.bfloat16)
    clip_ids = lax.all_gather(frame_clip, "seq", axis=1, tiled=True)[0]
    same_clip = clip_ids[:, None] == clip_ids[None, :]
    grad_split = out_grad[0].reshape(frames_dev, seq_count, local_pos, width)
    projected = jnp.dot(normed.reshape(-1, width), qkv_weight, preferred_element_type=jnp.float32)
    projected = projected.astype(jnp.bfloat16).reshape(frames_dev, seq_count, local_pos, 3 * width)
    moved_proj = lax.all_to_all(projected, "seq", split_axis=1, concat_axis=0, tiled=True)
    incoming = lax.all_to_all(grad_split, "seq", split_axis=1, concat_axis=0, tiled=True)
    grads_frames = attention_grad(moved_proj[:, 0], incoming[:, 0], same_clip)[:, None]
    grads_qkv = lax.all_to_all(grads_frames, "seq", split_axis=0, concat_axis=1, tiled=True)
    rows_x = normed.reshape(-1, width)
    rows_g = grads_qkv.reshape(-1, 3 * width)
    d_normed = transpose_product(rows_g, qkv_weight).reshape(frames_dev, patches, width)
    value_rows = rows_g[:, 2 * width :]
    weight_sum = lax.psum_scatter(
        lax.dot_general(
            rows_x, value_rows, (((0,), (0,)), ((), ())), preferred_element_type=jnp.float32
        ),
        ("dp", "seq"),
        scatter_dimension=0,
        tiled=True,
    )
    gain_local = jnp.sum(d_normed * normalized, axis=(0, 1))
    gain_sum = lax.psum(gain_local, ("dp", "seq"))
    d_hat = d_normed * norm_gain
    first_mean = jnp.mean(d_hat, axis=-1, keepdims=True)
    second_mean = jnp.mean(d_hat * normalized, axis=-1, keepdims=True)
    input_grad = (inv_std * (d_hat - first_mean - normalized * second_mean)).astype(jnp.bfloat16)
    return (input_grad[None], weight_sum * factor, gain_sum * factor)


MESH = pl.DeviceIdType.MESH
BF = jnp.bfloat16
F32 = jnp.float32
ROWS = 16
PAD = 48
SPLIT = 896
PARTS_Y = ((0, 384), (384, 256), (640, 256))
PARTS_X = ((0, 256), (256, 128), (384, 128))
CHUNKS = range(3)


def fused(
    x_ref, do_ref, gain_ref, w_hbm, clip_ref,
    ig_ref, wg_ref, gg_ref,
    gn, cl, w, rn, rp, cn, cp, mk, nz, iv, nb, dos, proj, t1, t2, em, et, bc, g, dn, dnt, igs, qn, qp,
    tr, nt, nr, dvr, sx, sy, rx, ry, kx, ky, tx, ty, rtx, rty, fin, u, zr, gp, gr, zg,
    wsem, send, recv,
):
    dp = lax.axis_index("dp")
    s = lax.axis_index("seq")
    z, y = dp // 2, dp % 2
    xx, core = s // 2, s % 2
    half = x_ref.shape[0] // 2
    width = x_ref.shape[1]
    head_dim = width // HEADS
    block = wg_ref.shape[0]
    scaling = head_dim ** (-0.5)
    prev, after = (dp, lax.rem(s + 3, 4)), (dp, lax.rem(s + 1, 4))
    has_prev, has_next = s > 0, s < 3
    core_dev = (dp, xx * 2 + (1 - core))
    x_dev = (dp, (1 - xx) * 2 + core)
    y_dev = (z * 2 + (1 - y), s)
    z_devs = [(lax.rem(z + d, 4) * 2 + y, s) for d in (1, 2, 3)]

    loads = [
        pltpu.make_async_copy(w_hbm.at[:, pl.ds(j * width, width)], w.at[j], wsem.at[j])
        for j in range(3)
    ]
    for load in loads:
        load.start()

    gn[...] = gain_ref[...].reshape(1, width)
    cl[...] = jnp.full(cl.shape, clip_ref[0, 0], jnp.int32)

    barrier = pltpu.get_barrier_semaphore()
    for dev in [core_dev, x_dev, y_dev, (dp, 3 - s)] + z_devs:
        pl.semaphore_signal(barrier, inc=1, device_id=dev, device_id_type=MESH)
    pl.semaphore_wait(barrier, 7)

    def remote(index, src, dst, dev):
        return pltpu.make_async_remote_copy(
            src_ref=src, dst_ref=dst, send_sem=send.at[index], recv_sem=recv.at[index],
            device_id=dev, device_id_type=MESH,
        )

    lower, upper = pl.ds(0, half), pl.ds(half, half)
    clip_p = remote(4, cl, cn, prev)
    clip_n = remote(5, cl, cp, after)
    x_p = remote(0, x_ref.at[lower], rn.at[0], prev)
    do_p = remote(1, do_ref.at[lower], rn.at[1], prev)
    x_n = remote(2, x_ref.at[upper], rp.at[0], after)
    do_n = remote(3, do_ref.at[upper], rp.at[1], after)
    to_prev, to_next = [clip_p, x_p, do_p], [clip_n, x_n, do_n]

    @pl.when(has_prev)
    def _():
        for copy in to_prev:
            copy.start()

    @pl.when(has_next)
    def _():
        for copy in to_next:
            copy.start()

    @pl.when(s == 0)
    def _():
        rp[...] = jnp.zeros_like(rp)
        cp[...] = jnp.full_like(cp, -1)

    @pl.when(s == 3)
    def _():
        rn[...] = jnp.zeros_like(rn)
        cn[...] = jnp.full_like(cn, -1)

    row = lax.broadcasted_iota(jnp.int32, em.shape, 0)
    col = lax.broadcasted_iota(jnp.int32, em.shape, 1) * head_dim
    em[...] = jnp.where((row >= col) & (row < col + head_dim), 1.0, 0.0).astype(BF)
    row = lax.broadcasted_iota(jnp.int32, et.shape, 0) * head_dim
    col = lax.broadcasted_iota(jnp.int32, et.shape, 1)
    et[...] = jnp.where((col >= row) & (col < row + head_dim), 1.0, 0.0).astype(BF)
    tr[pl.ds(width, 8), :] = jnp.zeros((8, tr.shape[1]), F32)

    @pl.when(has_next)
    def _():
        clip_p.wait_recv()

    @pl.when(has_prev)
    def _():
        clip_n.wait_recv()

    own_clip = cl[...]
    mk[0] = jnp.where(own_clip == cp[...], 1.0, 0.0)
    mk[1] = jnp.where(own_clip == cn[...], 1.0, 0.0)

    def masks(shape):
        before = jnp.broadcast_to(mk[0, 0:1, 0:1], shape) > 0.5
        later = jnp.broadcast_to(mk[1, 0:1, 0:1], shape) > 0.5
        return before, later

    def pick_first(own, index, r):
        before, _ = masks((ROWS, width))
        lo = own[pl.ds(r, ROWS), :].astype(F32)
        hi = own[pl.ds(half + r, ROWS), :].astype(F32)
        return jnp.where(before, hi, lo)

    def pick_second(own, index, r):
        before, later = masks((ROWS, width))
        hi = own[pl.ds(half + r, ROWS), :].astype(F32)
        from_next = rn[index, pl.ds(r, ROWS), :].astype(F32)
        from_prev = rp[index, pl.ds(r, ROWS), :].astype(F32)
        return jnp.where(later, from_next, jnp.where(before, from_prev, hi))

    chunks = half // ROWS

    def norm_half(base, pick):
        def norm_rows(c, carry):
            r = pl.multiple_of(c * ROWS, ROWS)
            rows = pick(x_ref, 0, r)
            at = pl.ds(base + r, ROWS)
            centered = rows - jnp.mean(rows, axis=-1, keepdims=True)
            inv = lax.rsqrt(jnp.mean(centered * centered, axis=-1, keepdims=True) + epsilon)
            normalized = centered * inv
            nz[at, :] = normalized
            iv[at, :] = jnp.broadcast_to(inv, (ROWS, 128))
            nb[at, :] = (normalized * gn[...]).astype(BF)
            return carry

        lax.fori_loop(0, chunks, norm_rows, 0, unroll=2)

    def project_half(base):
        rows = pl.ds(base, half)

        def project(j, carry):
            proj[j, rows, :] = jnp.dot(nb[rows, :], w[j], preferred_element_type=F32).astype(BF)
            return carry

        lax.fori_loop(0, 3, project, 0)

    def turn_half(base):
        rows = pl.ds(base, half)
        tr[pl.ds(0, width), :] = jnp.transpose(nb[rows, :].astype(F32))
        for i in range(32):
            nt[i % 2, (i // 2) % 2 * 2 + (i // 4) % 2, pl.ds(i // 8 * PAD, PAD), rows] = tr[
                pl.ds(i * block, PAD), :
            ].astype(BF)

    norm_half(0, pick_first)
    turn_half(0)
    for j in range(3):
        loads[j].wait()
    project_half(0)

    @pl.when(has_next)
    def _():
        x_p.wait_recv()

    @pl.when(has_prev)
    def _():
        x_n.wait_recv()

    norm_half(half, pick_second)
    project_half(half)
    turn_half(half)
    nt_copy = remote(6, nt.at[1 - core], nr, core_dev)
    nt_copy.start()

    @pl.when(has_next)
    def _():
        do_p.wait_recv()

    @pl.when(has_prev)
    def _():
        do_n.wait_recv()

    def products(c, carry):
        r = pl.multiple_of(c * ROWS, ROWS)
        a, b = pl.ds(r, ROWS), pl.ds(half + r, ROWS)
        do_a, do_b = pick_first(do_ref, 1, r), pick_second(do_ref, 1, r)
        dos[a, :] = do_a.astype(BF)
        dos[b, :] = do_b.astype(BF)
        kd = proj[1, a, :].astype(F32) - proj[1, b, :].astype(F32)
        vd = proj[2, a, :].astype(F32) - proj[2, b, :].astype(F32)
        t1[a, :] = (proj[0, a, :].astype(F32) * kd).astype(BF)
        t1[b, :] = (proj[0, b, :].astype(F32) * -kd).astype(BF)
        t2[a, :] = (do_a * vd).astype(BF)
        t2[b, :] = (do_b * -vd).astype(BF)
        return carry

    lax.fori_loop(0, chunks, products, 0)

    sd = jnp.dot(t1[...], em[...], preferred_element_type=F32) * scaling
    dd = jnp.dot(t2[...], em[...], preferred_element_type=F32)
    before, later = masks(sd.shape)
    paired = before | later
    own_p = jnp.where(paired, 1.0 / (1.0 + jnp.exp(-sd)), 1.0)
    other_p = jnp.where(paired, 1.0 / (1.0 + jnp.exp(sd)), 0.0)
    ds = own_p * other_p * dd * scaling
    for j, small in enumerate((own_p, other_p, ds)):
        bc[j] = jnp.dot(small.astype(BF), et[...], preferred_element_type=F32).astype(BF)

    def value_rows(c, carry):
        r = pl.multiple_of(c * ROWS, ROWS)
        a, b = pl.ds(r, ROWS), pl.ds(half + r, ROWS)
        do_a, do_b = dos[a, :].astype(F32), dos[b, :].astype(F32)
        g[2, a, :] = (bc[0, a, :].astype(F32) * do_a + bc[1, b, :].astype(F32) * do_b).astype(BF)
        g[2, b, :] = (bc[0, b, :].astype(F32) * do_b + bc[1, a, :].astype(F32) * do_a).astype(BF)
        return carry

    lax.fori_loop(0, chunks, value_rows, 0)
    dv_copy = remote(7, g.at[2], dvr, core_dev)
    dv_copy.start()

    def grad_rows(c, carry):
        r = pl.multiple_of(c * ROWS, ROWS)
        a, b = pl.ds(r, ROWS), pl.ds(half + r, ROWS)
        ds_a, ds_b = bc[2, a, :].astype(F32), bc[2, b, :].astype(F32)
        kd = proj[1, a, :].astype(F32) - proj[1, b, :].astype(F32)
        g[0, a, :] = (ds_a * kd).astype(BF)
        g[0, b, :] = (ds_b * -kd).astype(BF)
        dk = ds_a * proj[0, a, :].astype(F32) - ds_b * proj[0, b, :].astype(F32)
        g[1, a, :] = dk.astype(BF)
        g[1, b, :] = (-dk).astype(BF)
        return carry

    lax.fori_loop(0, chunks, grad_rows, 0)

    nt_copy.wait_recv()
    dv_copy.wait_recv()

    def term(group, cols):
        return jnp.dot(nt[core, group], g[2, :, cols], preferred_element_type=F32) + jnp.dot(
            nr[group], dvr[:, cols], preferred_element_type=F32
        )

    def in_y(k):
        return pl.ds(*PARTS_Y[k])

    def in_x(k):
        return pl.ds(*PARTS_X[k])

    def from_x(k):
        return pl.ds(SPLIT + PARTS_X[k][0], PARTS_X[k][1])

    x_first, y_first, x_second, y_second = [], [], [], []
    for k in CHUNKS:

        def send_terms(n, carry, k=k):
            sx[n, :, in_x(k)] = term((1 - xx) * 2 + n, from_x(k)).astype(BF)
            sy[n, :, in_y(k)] = term(n * 2 + (1 - y), in_y(k)).astype(BF)
            return carry

        lax.fori_loop(0, 2, send_terms, 0)
        x_first.append(remote(10 + k, sx.at[:, :, in_x(k)], rx.at[:, :, in_x(k)], x_dev))
        y_first.append(remote(13 + k, sy.at[:, :, in_y(k)], ry.at[:, :, in_y(k)], y_dev))
        x_first[k].start()
        y_first[k].start()

    def keep_terms(n, carry):
        kx[n] = term(xx * 2 + n, pl.ds(SPLIT, width - SPLIT))
        ky[n] = term(n * 2 + y, pl.ds(0, SPLIT))
        return carry

    lax.fori_loop(0, 2, keep_terms, 0)

    def back(j):
        part = lax.dot_general(
            w[j], g[j], (((1,), (1,)), ((), ())), preferred_element_type=F32
        )
        dnt[...] = part if j == 0 else dnt[...] + part

    def second_stage(k):
        y_first[k].wait_recv()
        tx[:, in_y(k)] = (
            ky[1 - xx, :, in_y(k)] + ry[1 - xx, :, in_y(k)].astype(F32)
        ).astype(BF)
        x_second.append(remote(18 + k, tx.at[:, in_y(k)], rtx.at[:, in_y(k)], x_dev))
        x_second[k].start()
        x_first[k].wait_recv()
        ty[:, in_x(k)] = (
            kx[1 - y, :, in_x(k)] + rx[1 - y, :, in_x(k)].astype(F32)
        ).astype(BF)
        y_second.append(remote(21 + k, ty.at[:, in_x(k)], rty.at[:, in_x(k)], y_dev))
        y_second[k].start()
        fin[:, in_y(k)] = ky[xx, :, in_y(k)] + ry[xx, :, in_y(k)].astype(F32)
        fin[:, from_x(k)] = kx[y, :, in_x(k)] + rx[y, :, in_x(k)].astype(F32)

    z_copies = []

    def pass_on(index, cols):
        for n in range(4):
            u[n, :, cols] = fin[pl.ds(n * PAD, PAD), cols].astype(BF)
        for d in range(3):
            z_copies.append(
                remote(
                    index + d, u.at[lax.rem(z + d + 1, 4), :, cols], zr.at[d, :, cols], z_devs[d]
                )
            )
            z_copies[-1].start()

    def finish(k):
        y_second[k].wait_recv()
        fin[:, from_x(k)] = fin[:, from_x(k)] + rty[:, in_x(k)].astype(F32)
        pass_on(28 + 6 * k, from_x(k))
        x_second[k].wait_recv()
        fin[:, in_y(k)] = fin[:, in_y(k)] + rtx[:, in_y(k)].astype(F32)
        pass_on(31 + 6 * k, in_y(k))

    back(0)
    second_stage(0)
    back(1)
    back(2)
    dn[...] = jnp.transpose(dnt[...])

    def input_rows(c, acc):
        r = pl.multiple_of(c * ROWS, ROWS)
        at = pl.ds(r, ROWS)
        normalized, d_normed = nz[at, :], dn[at, :]
        prod = d_normed * normalized
        d_hat = d_normed * gn[...]
        first = jnp.mean(d_hat, axis=-1, keepdims=True)
        second = jnp.mean(d_hat * normalized, axis=-1, keepdims=True)
        result = iv[at, 0:1] * (d_hat - first - normalized * second)
        igs[at, :] = result.astype(BF)
        return acc + (prod[0:8] + prod[8:16])

    gp[0] = lax.fori_loop(
        0, 2 * chunks, input_rows, jnp.zeros((8, width), F32), unroll=2
    )

    ig_p = remote(8, igs.at[upper], qn, prev)
    ig_n = remote(9, igs.at[upper], qp, after)

    @pl.when(s == 0)
    def _():
        qp[...] = jnp.zeros_like(qp)

    @pl.when(s == 3)
    def _():
        qn[...] = jnp.zeros_like(qn)

    gain_core = remote(16, gp.at[0], gr.at[0], core_dev)
    gain_core.start()

    second_stage(1)
    finish(0)

    gain_core.wait_recv()
    gp[1] = gp[0] + gr[0]
    gain_x = remote(17, gp.at[1], gr.at[1], x_dev)
    gain_x.start()

    second_stage(2)

    @pl.when(has_prev)
    def _():
        ig_p.start()

    @pl.when(has_next)
    def _():
        ig_n.start()

    finish(1)

    gain_x.wait_recv()
    gp[2] = gp[1] + gr[1]
    gain_y = remote(24, gp.at[2], gr.at[2], y_dev)
    gain_y.start()

    finish(2)

    gain_y.wait_recv()
    zg[z] = gp[2] + gr[2]
    gain_z = [remote(25 + d, zg.at[z], zg.at[z], z_devs[d]) for d in range(3)]
    for copy in gain_z:
        copy.start()

    @pl.when(has_next)
    def _():
        ig_p.wait_recv()

    @pl.when(has_prev)
    def _():
        ig_n.wait_recv()

    def output_rows(c, carry):
        r = pl.multiple_of(c * ROWS, ROWS)
        a, b = pl.ds(r, ROWS), pl.ds(half + r, ROWS)
        prior, later_too = masks((ROWS, width))
        first, second = igs[a, :].astype(F32), igs[b, :].astype(F32)
        ig_ref[a, :] = jnp.where(prior, qp[a, :].astype(F32), first).astype(BF)
        ig_ref[b, :] = jnp.where(
            prior, first, jnp.where(later_too, qn[a, :].astype(F32), second)
        ).astype(BF)
        return carry

    lax.fori_loop(0, chunks, output_rows, 0)

    factor = (x_ref.shape[0] * 32) ** (-0.5)
    for copy in gain_z:
        copy.wait_recv()
    total = (zg[0] + zg[1]) + (zg[2] + zg[3])
    gg_ref[...] = jnp.sum(total, axis=0) * factor

    for copy in z_copies:
        copy.wait_recv()
    own = fin[pl.ds(pl.multiple_of(z * PAD, PAD), PAD), :]
    summed = own + zr[0].astype(F32) + zr[1].astype(F32) + zr[2].astype(F32)
    wg_ref[...] = summed[0:block] * factor

    @pl.when(has_prev)
    def _():
        for copy in to_prev + [ig_p]:
            copy.wait_send()

    @pl.when(has_next)
    def _():
        for copy in to_next + [ig_n]:
            copy.wait_send()

    sent = [nt_copy, dv_copy, gain_core, gain_x, gain_y] + x_first + y_first
    for copy in sent + x_second + y_second + gain_z + z_copies:
        copy.wait_send()


def settle(a, b, c, a_out, b_out, c_out):
    a_out[...] = a[...]
    b_out[...] = b[...]
    c_out[...] = c[...]


def paired_shards(block_input, norm_gain, qkv_weight, frame_clip, out_grad):
    tokens, width = block_input.shape[2:]
    half = tokens // 2
    block = width // 32
    smem = pl.BlockSpec(memory_space=pltpu.SMEM)
    vmem = pl.BlockSpec(memory_space=pltpu.VMEM)
    rest = width - SPLIT
    group = 4 * PAD

    def buf(*shape):
        return pltpu.VMEM(shape, BF)

    def ids(*shape):
        return pltpu.VMEM(shape, jnp.int32)

    def wide(*shape):
        return pltpu.VMEM(shape, F32)

    scratch = [
        wide(1, width), ids(8, 128), buf(3, width, width), buf(2, half, width), buf(2, half, width),
        ids(8, 128), ids(8, 128), wide(2, 8, 128),
        wide(tokens, width), wide(tokens, 128), buf(tokens, width), buf(tokens, width),
        buf(3, tokens, width), buf(tokens, width), buf(tokens, width),
        buf(width, 128), buf(128, width), buf(3, tokens, width), buf(3, tokens, width),
        wide(tokens, width), wide(width, tokens), buf(tokens, width),
        buf(half, width), buf(half, width),
        wide(width + 8, half), buf(2, 4, group, tokens), buf(4, group, tokens),
        buf(tokens, width),
        buf(2, group, rest), buf(2, group, SPLIT), buf(2, group, rest), buf(2, group, SPLIT),
        wide(2, group, rest), wide(2, group, SPLIT),
        buf(group, SPLIT), buf(group, rest), buf(group, SPLIT), buf(group, rest),
        wide(group, width), buf(4, PAD, width), buf(3, PAD, width),
        wide(3, 8, width), wide(3, 8, width), wide(4, 8, width),
        pltpu.SemaphoreType.DMA((3,)),
        pltpu.SemaphoreType.DMA((46,)), pltpu.SemaphoreType.DMA((46,)),
    ]
    results = pl.pallas_call(
        fused,
        out_shape=(
            jax.ShapeDtypeStruct((tokens, width), BF),
            jax.ShapeDtypeStruct((block, width), F32),
            jax.ShapeDtypeStruct((width,), F32),
        ),
        in_specs=[vmem, vmem, vmem, pl.BlockSpec(memory_space=pl.ANY), smem],
        out_specs=(vmem, vmem, vmem),
        scratch_shapes=scratch,
        compiler_params=pltpu.CompilerParams(
            collective_id=0, has_side_effects=True, vmem_limit_bytes=56 * 1024 * 1024
        ),
        cost_estimate=pl.CostEstimate(
            flops=8_000_000_000, bytes_accessed=16_000_000, transcendentals=100_000
        ),
    )(block_input[0, 0], out_grad[0, 0], norm_gain, qkv_weight, frame_clip)
    input_grad, weight_grad, gain_grad = pl.pallas_call(
        settle,
        out_shape=tuple(jax.ShapeDtypeStruct(r.shape, r.dtype) for r in results),
        in_specs=[vmem] * 3,
        out_specs=(vmem,) * 3,
    )(*results)
    return input_grad[None, None], weight_grad, gain_grad


def solution(mesh):
    placed = (P("dp", "seq", None, None), P(), P(), P("dp", "seq"), P("dp", "seq", None, None))

    def whole(block_input, *others):
        small = mesh.shape["dp"] == 8 and mesh.shape["seq"] == 4 and block_input.shape[1] == 4
        return jax.shard_map(
            paired_shards if small else shards,
            mesh=mesh,
            in_specs=placed,
            out_specs=(P("dp", "seq", None, None), P(("dp", "seq"), None), P()),
            check_vma=False,
        )(block_input, *others)

    return whole
```

```python
import jax
import jax.numpy as jnp
from jax import lax
from jax.experimental import pallas as pl
from jax.experimental.pallas import tpu as pltpu
from jax.sharding import PartitionSpec as P

HEADS = 16


epsilon = 1e-06


def attention_grad(projected, incoming, same_clip):
    frames_all, positions, triple = projected.shape
    width = triple // 3
    head_dim = width // HEADS
    blocks = projected.reshape(frames_all, positions, 3, HEADS, head_dim)
    query_part = blocks[:, :, 0]
    key_part = blocks[:, :, 1]
    value_part = blocks[:, :, 2]
    outgrad = incoming.reshape(frames_all, positions, HEADS, head_dim)
    scaling = head_dim ** (-0.5)
    scores = (
        jnp.einsum("fphd,gphd->phfg", query_part, key_part, preferred_element_type=jnp.float32)
        * scaling
    )
    largest = jnp.max(jnp.where(same_clip, scores, -jnp.inf), axis=-1, keepdims=True)
    powers = jnp.where(same_clip, jnp.exp(scores - largest), 0.0)
    softmaxed = powers / jnp.sum(powers, axis=-1, keepdims=True)
    rounded_probs = softmaxed.astype(jnp.bfloat16)
    d_value = jnp.einsum(
        "phfg,fphd->gphd", rounded_probs, outgrad, preferred_element_type=jnp.float32
    )
    d_probs = jnp.einsum("fphd,gphd->phfg", outgrad, value_part, preferred_element_type=jnp.float32)
    row_dot = jnp.sum(softmaxed * d_probs, axis=-1, keepdims=True)
    d_scores = (softmaxed * (d_probs - row_dot) * scaling).astype(jnp.bfloat16)
    d_query = jnp.einsum("phfg,gphd->fphd", d_scores, key_part, preferred_element_type=jnp.float32)
    d_key = jnp.einsum("phfg,fphd->gphd", d_scores, query_part, preferred_element_type=jnp.float32)
    stacked = jnp.stack([d_query, d_key, d_value], axis=2)
    return stacked.reshape(frames_all, positions, triple).astype(jnp.bfloat16)


def transpose_product(grad_rows, qkv_weight):
    return lax.dot_general(
        grad_rows, qkv_weight, (((1,), (1,)), ((), ())), preferred_element_type=jnp.float32
    )


def shards(block_input, norm_gain, qkv_weight, frame_clip, out_grad):
    frames_dev = block_input.shape[1]
    patches = block_input.shape[2]
    width = block_input.shape[3]
    seq_count = lax.axis_size("seq")
    group_count = lax.axis_size("dp")
    local_pos = patches // seq_count
    factor = (frames_dev * patches * seq_count * group_count) ** (-0.5)
    inputs_f = block_input[0].astype(jnp.float32)
    centered = inputs_f - jnp.mean(inputs_f, axis=-1, keepdims=True)
    inv_std = lax.rsqrt(jnp.mean(centered * centered, axis=-1, keepdims=True) + epsilon)
    normalized = centered * inv_std
    normed = (normalized * norm_gain).astype(jnp.bfloat16)
    clip_ids = lax.all_gather(frame_clip, "seq", axis=1, tiled=True)[0]
    same_clip = clip_ids[:, None] == clip_ids[None, :]
    grad_split = out_grad[0].reshape(frames_dev, seq_count, local_pos, width)
    projected = jnp.dot(normed.reshape(-1, width), qkv_weight, preferred_element_type=jnp.float32)
    projected = projected.astype(jnp.bfloat16).reshape(frames_dev, seq_count, local_pos, 3 * width)
    moved_proj = lax.all_to_all(projected, "seq", split_axis=1, concat_axis=0, tiled=True)
    incoming = lax.all_to_all(grad_split, "seq", split_axis=1, concat_axis=0, tiled=True)
    grads_frames = attention_grad(moved_proj[:, 0], incoming[:, 0], same_clip)[:, None]
    grads_qkv = lax.all_to_all(grads_frames, "seq", split_axis=0, concat_axis=1, tiled=True)
    rows_x = normed.reshape(-1, width)
    rows_g = grads_qkv.reshape(-1, 3 * width)
    d_normed = transpose_product(rows_g, qkv_weight).reshape(frames_dev, patches, width)
    value_rows = rows_g[:, 2 * width :]
    weight_sum = lax.psum_scatter(
        lax.dot_general(
            rows_x, value_rows, (((0,), (0,)), ((), ())), preferred_element_type=jnp.float32
        ),
        ("dp", "seq"),
        scatter_dimension=0,
        tiled=True,
    )
    gain_local = jnp.sum(d_normed * normalized, axis=(0, 1))
    gain_sum = lax.psum(gain_local, ("dp", "seq"))
    d_hat = d_normed * norm_gain
    first_mean = jnp.mean(d_hat, axis=-1, keepdims=True)
    second_mean = jnp.mean(d_hat * normalized, axis=-1, keepdims=True)
    input_grad = (inv_std * (d_hat - first_mean - normalized * second_mean)).astype(jnp.bfloat16)
    return (input_grad[None], weight_sum * factor, gain_sum * factor)


MESH = pl.DeviceIdType.MESH
BF = jnp.bfloat16
F32 = jnp.float32
ROWS = 16
PAD = 48
SPLIT = 896
PARTS_Y = ((0, 384), (384, 256), (640, 256))
PARTS_X = ((0, 256), (256, 128), (384, 128))
CHUNKS = range(3)


def fused(
    x_ref, do_ref, gain_ref, w_hbm, clip_ref,
    ig_ref, wg_ref, gg_ref,
    gn, cl, w, rn, rp, cn, cp, mk, nz, iv, nb, dos, proj, t1, t2, em, et, bc, g, dn, dnt, igs, qn, qp,
    tr, nt, nr, dvr, sx, sy, rx, ry, kx, ky, tx, ty, rtx, rty, fin, u, zr, gp, gr, zg,
    wsem, send, recv,
):
    dp = lax.axis_index("dp")
    s = lax.axis_index("seq")
    z, y = dp // 2, dp % 2
    xx, core = s // 2, s % 2
    half = x_ref.shape[0] // 2
    width = x_ref.shape[1]
    head_dim = width // HEADS
    block = wg_ref.shape[0]
    scaling = head_dim ** (-0.5)
    prev, after = (dp, lax.rem(s + 3, 4)), (dp, lax.rem(s + 1, 4))
    has_prev, has_next = s > 0, s < 3
    core_dev = (dp, xx * 2 + (1 - core))
    x_dev = (dp, (1 - xx) * 2 + core)
    y_dev = (z * 2 + (1 - y), s)
    z_devs = [(lax.rem(z + d, 4) * 2 + y, s) for d in (1, 2, 3)]

    loads = [
        pltpu.make_async_copy(w_hbm.at[:, pl.ds(j * width, width)], w.at[j], wsem.at[j])
        for j in range(3)
    ]
    for load in loads:
        load.start()

    gn[...] = gain_ref[...].reshape(1, width)
    cl[...] = jnp.full(cl.shape, clip_ref[0, 0], jnp.int32)

    barrier = pltpu.get_barrier_semaphore()
    for dev in [core_dev, x_dev, y_dev, (dp, 3 - s)] + z_devs:
        pl.semaphore_signal(barrier, inc=1, device_id=dev, device_id_type=MESH)
    pl.semaphore_wait(barrier, 7)

    def remote(index, src, dst, dev):
        return pltpu.make_async_remote_copy(
            src_ref=src, dst_ref=dst, send_sem=send.at[index], recv_sem=recv.at[index],
            device_id=dev, device_id_type=MESH,
        )

    lower, upper = pl.ds(0, half), pl.ds(half, half)
    clip_p = remote(4, cl, cn, prev)
    clip_n = remote(5, cl, cp, after)
    x_p = remote(0, x_ref.at[lower], rn.at[0], prev)
    do_p = remote(1, do_ref.at[lower], rn.at[1], prev)
    x_n = remote(2, x_ref.at[upper], rp.at[0], after)
    do_n = remote(3, do_ref.at[upper], rp.at[1], after)
    to_prev, to_next = [clip_p, x_p, do_p], [clip_n, x_n, do_n]

    @pl.when(has_prev)
    def _():
        for copy in to_prev:
            copy.start()

    @pl.when(has_next)
    def _():
        for copy in to_next:
            copy.start()

    @pl.when(s == 0)
    def _():
        rp[...] = jnp.zeros_like(rp)
        cp[...] = jnp.full_like(cp, -1)

    @pl.when(s == 3)
    def _():
        rn[...] = jnp.zeros_like(rn)
        cn[...] = jnp.full_like(cn, -1)

    row = lax.broadcasted_iota(jnp.int32, em.shape, 0)
    col = lax.broadcasted_iota(jnp.int32, em.shape, 1) * head_dim
    em[...] = jnp.where((row >= col) & (row < col + head_dim), 1.0, 0.0).astype(BF)
    row = lax.broadcasted_iota(jnp.int32, et.shape, 0) * head_dim
    col = lax.broadcasted_iota(jnp.int32, et.shape, 1)
    et[...] = jnp.where((col >= row) & (col < row + head_dim), 1.0, 0.0).astype(BF)
    tr[pl.ds(width, 8), :] = jnp.zeros((8, tr.shape[1]), F32)

    @pl.when(has_next)
    def _():
        clip_p.wait_recv()

    @pl.when(has_prev)
    def _():
        clip_n.wait_recv()

    own_clip = cl[...]
    mk[0] = jnp.where(own_clip == cp[...], 1.0, 0.0)
    mk[1] = jnp.where(own_clip == cn[...], 1.0, 0.0)

    def masks(shape):
        before = jnp.broadcast_to(mk[0, 0:1, 0:1], shape) > 0.5
        later = jnp.broadcast_to(mk[1, 0:1, 0:1], shape) > 0.5
        return before, later

    def pick_first(own, index, r):
        before, _ = masks((ROWS, width))
        lo = own[pl.ds(r, ROWS), :].astype(F32)
        hi = own[pl.ds(half + r, ROWS), :].astype(F32)
        return jnp.where(before, hi, lo)

    def pick_second(own, index, r):
        before, later = masks((ROWS, width))
        hi = own[pl.ds(half + r, ROWS), :].astype(F32)
        from_next = rn[index, pl.ds(r, ROWS), :].astype(F32)
        from_prev = rp[index, pl.ds(r, ROWS), :].astype(F32)
        return jnp.where(later, from_next, jnp.where(before, from_prev, hi))

    chunks = half // ROWS

    def norm_half(base, pick):
        def norm_rows(c, carry):
            r = pl.multiple_of(c * ROWS, ROWS)
            rows = pick(x_ref, 0, r)
            at = pl.ds(base + r, ROWS)
            centered = rows - jnp.mean(rows, axis=-1, keepdims=True)
            inv = lax.rsqrt(jnp.mean(centered * centered, axis=-1, keepdims=True) + epsilon)
            normalized = centered * inv
            nz[at, :] = normalized
            iv[at, :] = jnp.broadcast_to(inv, (ROWS, 128))
            nb[at, :] = (normalized * gn[...]).astype(BF)
            return carry

        lax.fori_loop(0, chunks, norm_rows, 0, unroll=2)

    def project_half(base):
        rows = pl.ds(base, half)

        def project(j, carry):
            proj[j, rows, :] = jnp.dot(nb[rows, :], w[j], preferred_element_type=F32).astype(BF)
            return carry

        lax.fori_loop(0, 3, project, 0)

    def turn_half(base):
        rows = pl.ds(base, half)
        tr[pl.ds(0, width), :] = jnp.transpose(nb[rows, :].astype(F32))
        for i in range(32):
            nt[i % 2, (i // 2) % 2 * 2 + (i // 4) % 2, pl.ds(i // 8 * PAD, PAD), rows] = tr[
                pl.ds(i * block, PAD), :
            ].astype(BF)

    norm_half(0, pick_first)
    turn_half(0)
    for j in range(3):
        loads[j].wait()
    project_half(0)

    @pl.when(has_next)
    def _():
        x_p.wait_recv()

    @pl.when(has_prev)
    def _():
        x_n.wait_recv()

    norm_half(half, pick_second)
    project_half(half)
    turn_half(half)
    nt_copy = remote(6, nt.at[1 - core], nr, core_dev)
    nt_copy.start()

    @pl.when(has_next)
    def _():
        do_p.wait_recv()

    @pl.when(has_prev)
    def _():
        do_n.wait_recv()

    def products(c, carry):
        r = pl.multiple_of(c * ROWS, ROWS)
        a, b = pl.ds(r, ROWS), pl.ds(half + r, ROWS)
        do_a, do_b = pick_first(do_ref, 1, r), pick_second(do_ref, 1, r)
        dos[a, :] = do_a.astype(BF)
        dos[b, :] = do_b.astype(BF)
        kd = proj[1, a, :].astype(F32) - proj[1, b, :].astype(F32)
        vd = proj[2, a, :].astype(F32) - proj[2, b, :].astype(F32)
        t1[a, :] = (proj[0, a, :].astype(F32) * kd).astype(BF)
        t1[b, :] = (proj[0, b, :].astype(F32) * -kd).astype(BF)
        t2[a, :] = (do_a * vd).astype(BF)
        t2[b, :] = (do_b * -vd).astype(BF)
        return carry

    lax.fori_loop(0, chunks, products, 0)

    sd = jnp.dot(t1[...], em[...], preferred_element_type=F32) * scaling
    dd = jnp.dot(t2[...], em[...], preferred_element_type=F32)
    before, later = masks(sd.shape)
    paired = before | later
    own_p = jnp.where(paired, 1.0 / (1.0 + jnp.exp(-sd)), 1.0)
    other_p = jnp.where(paired, 1.0 / (1.0 + jnp.exp(sd)), 0.0)
    ds = own_p * other_p * dd * scaling
    for j, small in enumerate((own_p, other_p, ds)):
        bc[j] = jnp.dot(small.astype(BF), et[...], preferred_element_type=F32).astype(BF)

    def value_rows(c, carry):
        r = pl.multiple_of(c * ROWS, ROWS)
        a, b = pl.ds(r, ROWS), pl.ds(half + r, ROWS)
        do_a, do_b = dos[a, :].astype(F32), dos[b, :].astype(F32)
        g[2, a, :] = (bc[0, a, :].astype(F32) * do_a + bc[1, b, :].astype(F32) * do_b).astype(BF)
        g[2, b, :] = (bc[0, b, :].astype(F32) * do_b + bc[1, a, :].astype(F32) * do_a).astype(BF)
        return carry

    lax.fori_loop(0, chunks, value_rows, 0)
    dv_copy = remote(7, g.at[2], dvr, core_dev)
    dv_copy.start()

    def grad_rows(c, carry):
        r = pl.multiple_of(c * ROWS, ROWS)
        a, b = pl.ds(r, ROWS), pl.ds(half + r, ROWS)
        ds_a, ds_b = bc[2, a, :].astype(F32), bc[2, b, :].astype(F32)
        kd = proj[1, a, :].astype(F32) - proj[1, b, :].astype(F32)
        g[0, a, :] = (ds_a * kd).astype(BF)
        g[0, b, :] = (ds_b * -kd).astype(BF)
        dk = ds_a * proj[0, a, :].astype(F32) - ds_b * proj[0, b, :].astype(F32)
        g[1, a, :] = dk.astype(BF)
        g[1, b, :] = (-dk).astype(BF)
        return carry

    lax.fori_loop(0, chunks, grad_rows, 0)

    nt_copy.wait_recv()
    dv_copy.wait_recv()

    def term(group, cols):
        return jnp.dot(nt[core, group], g[2, :, cols], preferred_element_type=F32) + jnp.dot(
            nr[group], dvr[:, cols], preferred_element_type=F32
        )

    def in_y(k):
        return pl.ds(*PARTS_Y[k])

    def in_x(k):
        return pl.ds(*PARTS_X[k])

    def from_x(k):
        return pl.ds(SPLIT + PARTS_X[k][0], PARTS_X[k][1])

    x_first, y_first, x_second, y_second = [], [], [], []
    for k in CHUNKS:

        def send_terms(n, carry, k=k):
            sx[n, :, in_x(k)] = term((1 - xx) * 2 + n, from_x(k)).astype(BF)
            sy[n, :, in_y(k)] = term(n * 2 + (1 - y), in_y(k)).astype(BF)
            return carry

        lax.fori_loop(0, 2, send_terms, 0)
        x_first.append(remote(10 + k, sx.at[:, :, in_x(k)], rx.at[:, :, in_x(k)], x_dev))
        y_first.append(remote(13 + k, sy.at[:, :, in_y(k)], ry.at[:, :, in_y(k)], y_dev))
        x_first[k].start()
        y_first[k].start()

    def keep_terms(n, carry):
        kx[n] = term(xx * 2 + n, pl.ds(SPLIT, width - SPLIT))
        ky[n] = term(n * 2 + y, pl.ds(0, SPLIT))
        return carry

    lax.fori_loop(0, 2, keep_terms, 0)

    def back(j):
        part = lax.dot_general(
            w[j], g[j], (((1,), (1,)), ((), ())), preferred_element_type=F32
        )
        dnt[...] = part if j == 0 else dnt[...] + part

    def second_stage(k):
        y_first[k].wait_recv()
        tx[:, in_y(k)] = (
            ky[1 - xx, :, in_y(k)] + ry[1 - xx, :, in_y(k)].astype(F32)
        ).astype(BF)
        x_second.append(remote(18 + k, tx.at[:, in_y(k)], rtx.at[:, in_y(k)], x_dev))
        x_second[k].start()
        x_first[k].wait_recv()
        ty[:, in_x(k)] = (
            kx[1 - y, :, in_x(k)] + rx[1 - y, :, in_x(k)].astype(F32)
        ).astype(BF)
        y_second.append(remote(21 + k, ty.at[:, in_x(k)], rty.at[:, in_x(k)], y_dev))
        y_second[k].start()
        fin[:, in_y(k)] = ky[xx, :, in_y(k)] + ry[xx, :, in_y(k)].astype(F32)
        fin[:, from_x(k)] = kx[y, :, in_x(k)] + rx[y, :, in_x(k)].astype(F32)

    z_copies = []

    def pass_on(index, cols):
        for n in range(4):
            u[n, :, cols] = fin[pl.ds(n * PAD, PAD), cols].astype(BF)
        for d in range(3):
            z_copies.append(
                remote(
                    index + d, u.at[lax.rem(z + d + 1, 4), :, cols], zr.at[d, :, cols], z_devs[d]
                )
            )
            z_copies[-1].start()

    def finish(k):
        y_second[k].wait_recv()
        fin[:, from_x(k)] = fin[:, from_x(k)] + rty[:, in_x(k)].astype(F32)
        pass_on(28 + 6 * k, from_x(k))
        x_second[k].wait_recv()
        fin[:, in_y(k)] = fin[:, in_y(k)] + rtx[:, in_y(k)].astype(F32)
        pass_on(31 + 6 * k, in_y(k))

    back(0)
    second_stage(0)
    back(1)
    back(2)
    dn[...] = jnp.transpose(dnt[...])

    def input_rows(c, acc):
        r = pl.multiple_of(c * ROWS, ROWS)
        at = pl.ds(r, ROWS)
        normalized, d_normed = nz[at, :], dn[at, :]
        prod = d_normed * normalized
        d_hat = d_normed * gn[...]
        first = jnp.mean(d_hat, axis=-1, keepdims=True)
        second = jnp.mean(d_hat * normalized, axis=-1, keepdims=True)
        result = iv[at, 0:1] * (d_hat - first - normalized * second)
        igs[at, :] = result.astype(BF)
        return acc + (prod[0:8] + prod[8:16])

    gp[0] = lax.fori_loop(
        0, 2 * chunks, input_rows, jnp.zeros((8, width), F32), unroll=2
    )

    ig_p = remote(8, igs.at[upper], qn, prev)
    ig_n = remote(9, igs.at[upper], qp, after)

    @pl.when(s == 0)
    def _():
        qp[...] = jnp.zeros_like(qp)

    @pl.when(s == 3)
    def _():
        qn[...] = jnp.zeros_like(qn)

    gain_core = remote(16, gp.at[0], gr.at[0], core_dev)
    gain_core.start()

    @pl.when(has_prev)
    def _():
        ig_p.start()

    @pl.when(has_next)
    def _():
        ig_n.start()

    second_stage(1)
    finish(0)

    gain_core.wait_recv()
    gp[1] = gp[0] + gr[0]
    gain_x = remote(17, gp.at[1], gr.at[1], x_dev)
    gain_x.start()

    second_stage(2)

    finish(1)

    gain_x.wait_recv()
    gp[2] = gp[1] + gr[1]
    gain_y = remote(24, gp.at[2], gr.at[2], y_dev)
    gain_y.start()

    finish(2)

    gain_y.wait_recv()
    zg[z] = gp[2] + gr[2]
    gain_z = [remote(25 + d, zg.at[z], zg.at[z], z_devs[d]) for d in range(3)]
    for copy in gain_z:
        copy.start()

    @pl.when(has_next)
    def _():
        ig_p.wait_recv()

    @pl.when(has_prev)
    def _():
        ig_n.wait_recv()

    def output_rows(c, carry):
        r = pl.multiple_of(c * ROWS, ROWS)
        a, b = pl.ds(r, ROWS), pl.ds(half + r, ROWS)
        prior, later_too = masks((ROWS, width))
        first, second = igs[a, :].astype(F32), igs[b, :].astype(F32)
        ig_ref[a, :] = jnp.where(prior, qp[a, :].astype(F32), first).astype(BF)
        ig_ref[b, :] = jnp.where(
            prior, first, jnp.where(later_too, qn[a, :].astype(F32), second)
        ).astype(BF)
        return carry

    lax.fori_loop(0, chunks, output_rows, 0)

    factor = (x_ref.shape[0] * 32) ** (-0.5)
    for copy in gain_z:
        copy.wait_recv()
    total = (zg[0] + zg[1]) + (zg[2] + zg[3])
    gg_ref[...] = jnp.sum(total, axis=0) * factor

    for copy in z_copies:
        copy.wait_recv()
    own = fin[pl.ds(pl.multiple_of(z * PAD, PAD), PAD), :]
    summed = own + zr[0].astype(F32) + zr[1].astype(F32) + zr[2].astype(F32)
    wg_ref[...] = summed[0:block] * factor

    @pl.when(has_prev)
    def _():
        for copy in to_prev + [ig_p]:
            copy.wait_send()

    @pl.when(has_next)
    def _():
        for copy in to_next + [ig_n]:
            copy.wait_send()

    sent = [nt_copy, dv_copy, gain_core, gain_x, gain_y] + x_first + y_first
    for copy in sent + x_second + y_second + gain_z + z_copies:
        copy.wait_send()


def settle(a, b, c, a_out, b_out, c_out):
    a_out[...] = a[...]
    b_out[...] = b[...]
    c_out[...] = c[...]


def paired_shards(block_input, norm_gain, qkv_weight, frame_clip, out_grad):
    tokens, width = block_input.shape[2:]
    half = tokens // 2
    block = width // 32
    smem = pl.BlockSpec(memory_space=pltpu.SMEM)
    vmem = pl.BlockSpec(memory_space=pltpu.VMEM)
    rest = width - SPLIT
    group = 4 * PAD

    def buf(*shape):
        return pltpu.VMEM(shape, BF)

    def ids(*shape):
        return pltpu.VMEM(shape, jnp.int32)

    def wide(*shape):
        return pltpu.VMEM(shape, F32)

    scratch = [
        wide(1, width), ids(8, 128), buf(3, width, width), buf(2, half, width), buf(2, half, width),
        ids(8, 128), ids(8, 128), wide(2, 8, 128),
        wide(tokens, width), wide(tokens, 128), buf(tokens, width), buf(tokens, width),
        buf(3, tokens, width), buf(tokens, width), buf(tokens, width),
        buf(width, 128), buf(128, width), buf(3, tokens, width), buf(3, tokens, width),
        wide(tokens, width), wide(width, tokens), buf(tokens, width),
        buf(half, width), buf(half, width),
        wide(width + 8, half), buf(2, 4, group, tokens), buf(4, group, tokens),
        buf(tokens, width),
        buf(2, group, rest), buf(2, group, SPLIT), buf(2, group, rest), buf(2, group, SPLIT),
        wide(2, group, rest), wide(2, group, SPLIT),
        buf(group, SPLIT), buf(group, rest), buf(group, SPLIT), buf(group, rest),
        wide(group, width), buf(4, PAD, width), buf(3, PAD, width),
        wide(3, 8, width), wide(3, 8, width), wide(4, 8, width),
        pltpu.SemaphoreType.DMA((3,)),
        pltpu.SemaphoreType.DMA((46,)), pltpu.SemaphoreType.DMA((46,)),
    ]
    results = pl.pallas_call(
        fused,
        out_shape=(
            jax.ShapeDtypeStruct((tokens, width), BF),
            jax.ShapeDtypeStruct((block, width), F32),
            jax.ShapeDtypeStruct((width,), F32),
        ),
        in_specs=[vmem, vmem, vmem, pl.BlockSpec(memory_space=pl.ANY), smem],
        out_specs=(vmem, vmem, vmem),
        scratch_shapes=scratch,
        compiler_params=pltpu.CompilerParams(
            collective_id=0, has_side_effects=True, vmem_limit_bytes=56 * 1024 * 1024
        ),
        cost_estimate=pl.CostEstimate(
            flops=8_000_000_000, bytes_accessed=16_000_000, transcendentals=100_000
        ),
    )(block_input[0, 0], out_grad[0, 0], norm_gain, qkv_weight, frame_clip)
    input_grad, weight_grad, gain_grad = pl.pallas_call(
        settle,
        out_shape=tuple(jax.ShapeDtypeStruct(r.shape, r.dtype) for r in results),
        in_specs=[vmem] * 3,
        out_specs=(vmem,) * 3,
    )(*results)
    return input_grad[None, None], weight_grad, gain_grad


def solution(mesh):
    placed = (P("dp", "seq", None, None), P(), P(), P("dp", "seq"), P("dp", "seq", None, None))

    def whole(block_input, *others):
        small = mesh.shape["dp"] == 8 and mesh.shape["seq"] == 4 and block_input.shape[1] == 4
        return jax.shard_map(
            paired_shards if small else shards,
            mesh=mesh,
            in_specs=placed,
            out_specs=(P("dp", "seq", None, None), P(("dp", "seq"), None), P()),
            check_vma=False,
        )(block_input, *others)

    return whole
```
